32 devices in a mesh: dp: 8 (over z, x), tensor: 4 (over y, core).
Axes of the slice: x: 2, y: 2, z: 4, core: 2. Of those that a mesh axis runs over, the one named last changes fastest.
Arguments:
- hidden_in: bfloat16 [16384, 1024], P(('dp', 'tensor')), may hold values from -6 to 6
- norm_gain: float32 [2, 1024], replicated, may hold values from 0.5 to 1.5
- norm_shift: float32 [2, 1024], replicated, may hold values from -2 to 2
- qkv_weight: bfloat16 [3, 1024, 1024], P(None, 'dp', 'tensor'), may hold values from -0.1875 to 0.1875
- qv_bias: float32 [2, 1024], P(None, 'tensor'), may hold values from -2 to 2
- out_weight: bfloat16 [1024, 1024], P('tensor', 'dp'), may hold values from -0.75 to 0.75
- out_bias: float32 [2, 1024], replicated, may hold values from -2 to 2
- up_weight: bfloat16 [1024, 4096], P('dp', 'tensor'), may hold values from -0.1875 to 0.1875
- up_bias: float32 [4096], P('tensor'), may hold values from -2 to 2
- down_weight: bfloat16 [4096, 1024], P('tensor', 'dp'), may hold values from -0.09375 to 0.09375
- cotangent: bfloat16 [16384, 1024], P(('dp', 'tensor')), may hold values from -6 to 6
Outputs:
- block_out: float32 [16384, 1024], P(('dp', 'tensor'))
- grad_in: float32 [16384, 1024], P(('dp', 'tensor'))
- grad_norm_gain: float32 [2, 1024], replicated
- grad_norm_shift: float32 [2, 1024], replicated
- grad_qkv: float32 [3, 1024, 1024], P(None, 'dp', 'tensor')
- grad_qv_bias: float32 [2, 1024], P(None, 'tensor')
- grad_out_weight: float32 [1024, 1024], P('tensor', 'dp')
- grad_out_bias: float32 [2, 1024], replicated
- grad_up_weight: float32 [1024, 4096], P('dp', 'tensor')
- grad_up_bias: float32 [4096], P('tensor')
- grad_down_weight: float32 [4096, 1024], P('tensor', 'dp')
The draws below stay inside these ranges and needn't reach their ends.
All inputs are finite; a program needn't handle non-finite values.
Results may differ from the reference program's by a relative error of at most 0.014.
Values may be sent and summed in bfloat16 or wider, within the bound.
No kernel may reach another device: no remote copies, remote signals or barrier semaphores. Data moves between devices by JAX's collectives and lax.ppermute only.
A program may use at most 192 MiB of HBM per device.

```python
import math
import jax
import jax.numpy as jnp
from jax import lax

D = 1024
HEADS = 16
FF = 4096
LEN = 2048
TOKENS = 16384


def level_of(own_key, dims, split, smallest, high):
    def one(axis_at, blocks):
        heights = jax.random.uniform(jax.random.fold_in(jax.random.fold_in(own_key, 6), axis_at), (blocks,), jnp.float32, smallest / len(split), high / len(split))
        return jnp.repeat(jnp.exp(heights), dims[axis_at] // blocks).reshape((-1,) + (1,) * (len(dims) - axis_at - 1))

    factor_of = one(*split[0])
    for cut in split[1:]:
        factor_of = factor_of * one(*cut)
    return factor_of


def centred(key, dims, deviation, reach, pieces=(), held_as=jnp.bfloat16):
    result = jax.random.normal(key, dims, jnp.float32) * deviation
    if len(pieces) > 0:
        result = level_of(key, dims, pieces, -0.22, 0.18) * result
    return jnp.clip(result, min=-reach, max=reach).astype(held_as)


def setup_inputs(seed: int = 0) -> dict:
    keys = jax.random.split(jax.random.key(seed), 12)
    return {
        "hidden_in": centred(keys[0], (TOKENS, D), 1.0, 6.0, ((0, 32),)),
        "norm_gain": jnp.clip(1.0 + 0.1 * jax.random.normal(keys[1], (2, D), jnp.float32), 0.5, 1.5),
        "norm_shift": centred(keys[2], (2, D), 0.3, 2.0, (), jnp.float32),
        "qkv_weight": centred(keys[3], (3, D, D), D ** -0.5, 0.1875, ((1, 8), (2, 4))),
        "qv_bias": centred(keys[4], (2, D), 0.3, 2.0, ((1, 4),), jnp.float32),
        "out_weight": centred(keys[5], (D, D), (D // 16) ** -0.5, 0.75, ((0, 4), (1, 8))),
        "out_bias": centred(keys[6], (2, D), 0.3, 2.0, (), jnp.float32),
        "up_weight": centred(keys[7], (D, FF), D ** -0.5, 0.1875, ((0, 8), (1, 4))),
        "up_bias": centred(keys[8], (FF,), 0.3, 2.0, ((0, 4),), jnp.float32),
        "down_weight": centred(keys[9], (FF, D), FF ** -0.5, 0.09375, ((0, 4), (1, 8))),
        "cotangent": centred(keys[10], (TOKENS, D), 1.0, 6.0, ((0, 32),)),
    }


precise = lax.Precision.HIGHEST

@jax.custom_vjp
def low(v):
    return lax.optimization_barrier(v.astype(jnp.bfloat16)).astype(jnp.float32)

@jax.custom_vjp
def low_back(v):
    return v

def low_keep(v):
    return (low(v), None)

def low_pass(kept, grad):
    return (grad,)

def back_keep(v):
    return (v, None)

def back_low(kept, grad):
    return (low(grad),)
low.defvjp(low_keep, low_pass)
low_back.defvjp(back_keep, back_low)

def round_both(values):
    return low(low_back(values))

def layer_norm(values, norm_gain, norm_shift):
    average = lax.optimization_barrier(jnp.mean(values, axis=-1, keepdims=True))
    centered = values - average
    inverse = lax.rsqrt(lax.optimization_barrier(jnp.mean(centered * centered, axis=-1, keepdims=True)) + 1e-05)
    return centered * inverse * norm_gain + norm_shift

def gelu_tanh(values):
    tanh_input = 0.7978845608 * (values + 0.044715 * values * values * values)
    return 0.5 * values * (1.0 + jnp.tanh(tanh_input))

def sequence_attention(queries, key_rows, value_rows):
    head_dim = D // HEADS
    block_rows = min(512, LEN)
    query_heads = queries.reshape(LEN, HEADS, head_dim)
    key_heads = key_rows.reshape(LEN, HEADS, head_dim)
    value_heads = value_rows.reshape(LEN, HEADS, head_dim)
    slopes = jnp.exp2(-8.0 * (jnp.arange(HEADS).astype(jnp.float32) + 1.0) / HEADS)

    @jax.checkpoint
    def one_block(block_index):
        offset = (block_index * block_rows).astype(jnp.int32)
        query_block = lax.dynamic_slice_in_dim(query_heads, offset, block_rows, 0)
        raw_scores = jnp.einsum('qhd,khd->hqk', query_block, key_heads, precision=precise)
        query_pos = offset + lax.broadcasted_iota(jnp.int32, (block_rows, LEN), 0)
        key_pos = lax.broadcasted_iota(jnp.int32, (block_rows, LEN), 1)
        distance = query_pos - key_pos
        scores = low_back(raw_scores * (1.0 / math.sqrt(head_dim)) - slopes[:, None, None] * distance.astype(jnp.float32)[None])
        masked = jnp.where((distance >= 0)[None], scores, -1000000000.0)
        maxima = lax.optimization_barrier(jnp.max(masked, axis=-1, keepdims=True))
        weights = jnp.exp(masked - maxima)
        attention = low(weights / lax.optimization_barrier(jnp.sum(weights, axis=-1, keepdims=True)))
        mixed_block = jnp.einsum('hqk,khd->qhd', attention, value_heads, precision=precise)
        return mixed_block.reshape(block_rows, D)
    blocks = lax.map(one_block, jnp.arange(LEN // block_rows, dtype=jnp.int32))
    return blocks.reshape(LEN, D)

def forward(hidden, norm_gain, norm_shift, qkv_weight, qv_bias, out_weight, out_bias, up_weight, up_bias, down_weight):
    normed = low(layer_norm(hidden, norm_gain[0], norm_shift[0]))
    queries = round_both(jnp.dot(normed, qkv_weight[0], precision=precise) + qv_bias[0])
    key_rows = round_both(jnp.dot(normed, qkv_weight[1], precision=precise))
    value_rows = round_both(jnp.dot(normed, qkv_weight[2], precision=precise) + qv_bias[1])
    sequences = TOKENS // LEN

    def per_sequence(items):
        return sequence_attention(items[0], items[1], items[2])
    mixed = lax.map(per_sequence, (queries.reshape(sequences, LEN, D), key_rows.reshape(sequences, LEN, D), value_rows.reshape(sequences, LEN, D)))
    mixed = round_both(mixed.reshape(TOKENS, D))
    middle = hidden + low_back(jnp.dot(mixed, out_weight, precision=precise)) + out_bias[0]
    second = low(layer_norm(middle, norm_gain[1], norm_shift[1]))
    upper = low_back(jnp.dot(second, up_weight, precision=precise) + up_bias)
    active = low(gelu_tanh(upper))
    return middle + low_back(jnp.dot(active, down_weight, precision=precise)) + out_bias[1]

def reference(hidden_in, norm_gain, norm_shift, qkv_weight, qv_bias, out_weight, out_bias, up_weight, up_bias, down_weight, cotangent):
    floats = (hidden_in.astype(jnp.float32), norm_gain, norm_shift, qkv_weight.astype(jnp.float32), qv_bias, out_weight.astype(jnp.float32), out_bias, up_weight.astype(jnp.float32), up_bias, down_weight.astype(jnp.float32))
    block_out, pullback = jax.vjp(forward, *floats)
    grads = pullback(cotangent.astype(jnp.float32))
    return (block_out, grads[0], grads[1], grads[2], grads[3], grads[4], grads[5], grads[6], grads[7], grads[8], grads[9])
```

```python
import functools
import math

import jax
import jax.numpy as jnp
from jax import lax
from jax.experimental import pallas as pl
from jax.experimental.pallas import tpu as pltpu
from jax.sharding import PartitionSpec as P

HEADS = 16
LOG2E = 1.4426950408889634
NEG = -1e30
BF16 = jnp.bfloat16
F32 = jnp.float32


def layer_norm(values, norm_gain, norm_shift):
    average = jnp.mean(values, axis=-1, keepdims=True)
    centered = values - average
    inverse = lax.rsqrt(jnp.mean(centered * centered, axis=-1, keepdims=True) + 1e-05)
    scaled = centered * inverse
    return (scaled * norm_gain + norm_shift, scaled, inverse)


def norm_backward(gradient, scaled, inverse, norm_gain):
    grad_scaled = gradient * norm_gain
    grad_mean = jnp.mean(grad_scaled, axis=-1, keepdims=True)
    grad_proj = jnp.mean(grad_scaled * scaled, axis=-1, keepdims=True)
    grad_input = inverse * (grad_scaled - grad_mean - scaled * grad_proj)
    return (grad_input, jnp.sum(gradient * scaled, axis=0), jnp.sum(gradient, axis=0))


def gelu_both(values):
    square = values * values
    tangent = jnp.tanh(0.7978845608 * values * (1.0 + 0.044715 * square))
    half = 0.5 * (1.0 + tangent)
    slope = half + 0.5 * values * (1.0 - tangent * tangent) * 0.7978845608 * (
        1.0 + 3.0 * 0.044715 * square
    )
    return values * half, slope


def fill_bias(bias, masked, slope):
    size = bias.shape[0]
    key = lax.broadcasted_iota(jnp.int32, (size, size), 0)
    query = lax.broadcasted_iota(jnp.int32, (size, size), 1)
    value = key.astype(F32) * slope
    bias[...] = value
    masked[...] = jnp.where(key <= query, value, NEG)


def head_rows(block, head):
    half = block.shape[0] // 2
    rows = lax.broadcasted_iota(jnp.int32, block.shape, 0)
    keep = (rows < half) if head == 0 else (rows >= half)
    return jnp.where(keep, block, jnp.zeros_like(block))


def forward_kernel(
    place, slope_ref, q_ref, k_ref, v_ref, mixed_ref, full_ref, log_ref, bias, masked, values_t, *, scale
):
    pair = pl.program_id(0)
    query_block = pl.program_id(1)
    me = place[0]
    size = bias.shape[1]
    half = q_ref.shape[0] // 2

    @pl.when(query_block == 0)
    def _():
        values_t[...] = v_ref[...].T
        for head in range(2):
            fill_bias(bias.at[head], masked.at[head], slope_ref[2 * pair + head])

    outputs = []
    logs = []
    for head in range(2):
        step = slope_ref[2 * pair + head] * size
        queries = head_rows(q_ref[...], head)

        def block(key_block, carry, bias_block, head=head, step=step, queries=queries):
            top, total, acc = carry
            at = pl.multiple_of((key_block ^ me) * size, size)
            raw = jnp.dot(k_ref[pl.ds(at, size), :], queries, preferred_element_type=F32)
            scores = raw * scale + bias_block
            base = key_block.astype(F32) * step
            new_top = jnp.maximum(top, jnp.max(scores, axis=0, keepdims=True) + base)
            weights = jnp.exp2(scores - (new_top - base))
            fade = jnp.exp2(top - new_top)
            total = total * fade + jnp.sum(weights, axis=0, keepdims=True)
            rows = values_t[head * half : (head + 1) * half, pl.ds(at, size)]
            acc = acc * fade + jnp.dot(rows, weights.astype(BF16), preferred_element_type=F32)
            return new_top, total, acc

        start = (
            jnp.full((1, size), NEG, F32),
            jnp.zeros((1, size), F32),
            jnp.zeros((half, size), F32),
        )
        carry = lax.fori_loop(
            0, query_block, lambda i, c, head=head, block=block: block(i, c, bias[head]), start
        )
        top, total, acc = block(query_block, carry, masked[head])
        outputs.append(acc / total)
        logs.append(top + jnp.log2(total))
    result = jnp.concatenate(outputs, axis=0)
    full_ref[...] = result
    mixed_ref[...] = result.astype(BF16)
    log_ref[0] = jnp.concatenate(logs, axis=0)


def backward_kernel(
    place,
    slope_ref,
    q_ref,
    k_ref,
    v_ref,
    g_ref,
    full_ref,
    log_ref,
    gq_ref,
    gk_ref,
    gv_ref,
    bias,
    masked,
    gq_acc,
    delta,
    *,
    scale,
    factor,
):
    pair = pl.program_id(0)
    key_block = pl.program_id(1)
    blocks = pl.num_programs(1)
    me = place[0]
    size = bias.shape[1]
    half = q_ref.shape[0] // 2

    @pl.when(key_block == 0)
    def _():
        gq_acc[...] = jnp.zeros_like(gq_acc)
        for head in range(2):
            fill_bias(bias.at[head], masked.at[head], slope_ref[2 * pair + head])
            rows = slice(head * half, (head + 1) * half)
            delta[head : head + 1, :] = jnp.sum(
                g_ref[rows, :].astype(F32) * full_ref[rows, :], axis=0, keepdims=True
            )

    keys = k_ref[...]
    keys_t = keys.T
    values = v_ref[...]
    grad_k = jnp.zeros(keys.shape, F32)
    grad_v = jnp.zeros(keys.shape, F32)
    for head in range(2):
        base = key_block.astype(F32) * (slope_ref[2 * pair + head] * size)
        rows = slice(head * half, (head + 1) * half)

        def block(query_block, carry, bias_block, head=head, base=base, rows=rows):
            grad_k, grad_v = carry
            at = pl.multiple_of((query_block ^ me) * size, size)
            queries = head_rows(q_ref[:, pl.ds(at, size)], head)
            grads = head_rows(g_ref[:, pl.ds(at, size)], head)
            raw = jnp.dot(keys, queries, preferred_element_type=F32)
            log = log_ref[0, head : head + 1, pl.ds(at, size)] - base
            weights = jnp.exp2(raw * scale + (bias_block - log))
            along = jnp.dot(values, grads, preferred_element_type=F32)
            change = (weights * (along - delta[head : head + 1, pl.ds(at, size)])).astype(BF16)
            contract = (((1,), (1,)), ((), ()))
            grad_v = grad_v + lax.dot_general(
                weights.astype(BF16), grads, contract, preferred_element_type=F32
            )
            grad_k = grad_k + lax.dot_general(change, queries, contract, preferred_element_type=F32)
            gq_acc[rows, pl.ds(at, size)] += jnp.dot(
                keys_t[rows, :], change, preferred_element_type=F32
            )
            return grad_k, grad_v

        carry = block(key_block, (grad_k, grad_v), masked[head])
        grad_k, grad_v = lax.fori_loop(
            key_block + 1, blocks, lambda i, c, head=head, block=block: block(i, c, bias[head]), carry
        )
    gk_ref[...] = (grad_k * factor).astype(BF16)
    gv_ref[...] = grad_v.astype(BF16)

    @pl.when(key_block == blocks - 1)
    def _():
        gq_ref[...] = (gq_acc[...] * factor).astype(BF16)


def attend_forward(place, slopes, queries_t, keys, values, size, head_dim):
    width, length = queries_t.shape
    wide = 2 * head_dim
    pairs, blocks = width // wide, length // size
    along_q = pl.BlockSpec((wide, size), lambda p, i, me, s: (p, i ^ me[0]))
    whole = pl.BlockSpec((length, wide), lambda p, i, me, s: (0, p))
    return pl.pallas_call(
        functools.partial(forward_kernel, scale=LOG2E / math.sqrt(head_dim)),
        grid_spec=pltpu.PrefetchScalarGridSpec(
            num_scalar_prefetch=2,
            grid=(pairs, blocks),
            in_specs=[along_q, whole, whole],
            out_specs=[
                along_q,
                along_q,
                pl.BlockSpec((1, 2, size), lambda p, i, me, s: (p, 0, i ^ me[0])),
            ],
            scratch_shapes=[
                pltpu.VMEM((2, size, size), F32),
                pltpu.VMEM((2, size, size), F32),
                pltpu.VMEM((wide, length), BF16),
            ],
        ),
        out_shape=[
            jax.ShapeDtypeStruct((width, length), BF16),
            jax.ShapeDtypeStruct((width, length), F32),
            jax.ShapeDtypeStruct((pairs, 2, length), F32),
        ],
        compiler_params=pltpu.CompilerParams(vmem_limit_bytes=48 * 2**20),
        cost_estimate=pl.CostEstimate(
            flops=20 * 10**9, bytes_accessed=8 * 2**20, transcendentals=10**7
        ),
        name="attend_forward",
    )(place, slopes, queries_t, keys, values)


def attend_backward(place, slopes, queries_t, keys, values, grads_t, full, logs, size, head_dim):
    width, length = queries_t.shape
    wide = 2 * head_dim
    pairs, blocks = width // wide, length // size
    along_k = pl.BlockSpec((size, wide), lambda p, i, me, s: (i ^ me[0], p))
    whole = pl.BlockSpec((wide, length), lambda p, i, me, s: (p, 0))
    return pl.pallas_call(
        functools.partial(
            backward_kernel, scale=LOG2E / math.sqrt(head_dim), factor=1.0 / math.sqrt(head_dim)
        ),
        grid_spec=pltpu.PrefetchScalarGridSpec(
            num_scalar_prefetch=2,
            grid=(pairs, blocks),
            in_specs=[
                whole,
                along_k,
                along_k,
                whole,
                whole,
                pl.BlockSpec((1, 2, length), lambda p, i, me, s: (p, 0, 0)),
            ],
            out_specs=[whole, along_k, along_k],
            scratch_shapes=[
                pltpu.VMEM((2, size, size), F32),
                pltpu.VMEM((2, size, size), F32),
                pltpu.VMEM((wide, length), F32),
                pltpu.VMEM((2, length), F32),
            ],
        ),
        out_shape=[
            jax.ShapeDtypeStruct((width, length), BF16),
            jax.ShapeDtypeStruct((length, width), BF16),
            jax.ShapeDtypeStruct((length, width), BF16),
        ],
        compiler_params=pltpu.CompilerParams(vmem_limit_bytes=48 * 2**20),
        cost_estimate=pl.CostEstimate(
            flops=40 * 10**9, bytes_accessed=12 * 2**20, transcendentals=10**7
        ),
        name="attend_backward",
    )(place, slopes, queries_t, keys, values, grads_t, full, logs)


def swap(value, axis, distance):
    size = lax.axis_size(axis)
    return lax.ppermute(value, axis, [(i, i ^ distance) for i in range(size)])


def gather_blocks(value):
    far = swap(value, "tensor", 2)
    near = swap(value, "tensor", 1)
    return [value, near, far, swap(far, "tensor", 1)]


def scatter_blocks(parts):
    far = parts[2].astype(F32) + swap(parts[3], "tensor", 1).astype(F32)
    near = parts[0].astype(F32) + swap(parts[1], "tensor", 1).astype(F32)
    return near + swap(far.astype(BF16), "tensor", 2).astype(F32)


def exchange_blocks(parts):
    return [parts[0]] + [swap(parts[j], "tensor", j) for j in range(1, 4)]


def sum_over(value, axes):
    for axis in axes:
        distance = 1
        while distance < lax.axis_size(axis):
            value = value + swap(value, axis, distance)
            distance *= 2
    return value


def rows_of(value, count):
    size = value.shape[0] // count
    return [value[i * size : (i + 1) * size] for i in range(count)]


def dot(a, b, ca, cb):
    return lax.dot_general(a, b, (((ca,), (cb,)), ((), ())), preferred_element_type=F32)


def body(
    hidden_in,
    norm_gain,
    norm_shift,
    qkv_weight,
    qv_bias,
    out_weight,
    out_bias,
    up_weight,
    up_bias,
    down_weight,
    cotangent,
):
    local_rows = hidden_in.shape[0]
    tensor_size = lax.axis_size("tensor")
    dp_size = lax.axis_size("dp")
    local_width = qkv_weight.shape[2]
    local_heads = HEADS // tensor_size
    head_dim = local_width // local_heads
    me = lax.axis_index("tensor").astype(jnp.int32)
    place = me.reshape(1)
    head_ids = me * local_heads + jnp.arange(local_heads, dtype=jnp.int32)
    slopes = jnp.exp2(-8.0 * (head_ids.astype(F32) + 1.0) / HEADS) * LOG2E

    qkv_full = lax.all_gather(qkv_weight, "dp", axis=1, tiled=True)
    out_mine = lax.all_gather(out_weight, "dp", axis=1, tiled=True)
    up_full = lax.all_gather(up_weight, "dp", axis=0, tiled=True)
    down_full = lax.all_gather(down_weight, "dp", axis=1, tiled=True)

    hidden = hidden_in.astype(F32)
    normed, scaled_one, inverse_one = layer_norm(hidden, norm_gain[0], norm_shift[0])
    normed_rows = jnp.concatenate(gather_blocks(normed.astype(BF16)), axis=0)
    grad_rows = jnp.concatenate(gather_blocks(cotangent), axis=0)
    out_full = jnp.concatenate(gather_blocks(out_mine), axis=0)

    queries_t = (dot(qkv_full[0], normed_rows, 0, 1) + qv_bias[0][:, None]).astype(BF16)
    keys = dot(normed_rows, qkv_full[1], 1, 0).astype(BF16)
    values = (dot(normed_rows, qkv_full[2], 1, 0) + qv_bias[1]).astype(BF16)
    mixed_t, mixed_full, logs = attend_forward(
        place, slopes, queries_t, keys, values, local_rows, head_dim
    )
    mixed_parts = [
        mixed_t[:, j * local_rows : (j + 1) * local_rows] for j in range(tensor_size)
    ]
    mixed_all = jnp.concatenate(exchange_blocks(mixed_parts), axis=0)
    middle = hidden + dot(mixed_all, out_full, 0, 0) + out_bias[0]
    second, scaled_two, inverse_two = layer_norm(middle, norm_gain[1], norm_shift[1])
    second_rows = jnp.concatenate(gather_blocks(second.astype(BF16)), axis=0)

    upper = dot(second_rows, up_full, 1, 0) + up_bias
    active, slope = gelu_both(upper)
    active = active.astype(BF16)
    mlp_partial = dot(active, down_full, 1, 0).astype(BF16)
    grad_active = dot(grad_rows, down_full, 1, 1)
    grad_upper = (grad_active * slope).astype(BF16)
    second_partial = dot(grad_upper, up_full, 1, 1).astype(BF16)
    grad_second = scatter_blocks(rows_of(second_partial, tensor_size))
    mlp_sum = scatter_blocks(rows_of(mlp_partial, tensor_size))
    block_out = middle + mlp_sum + out_bias[1]

    grad_up_bias = jnp.sum(grad_upper.astype(F32), axis=0)
    grad_down = dot(active, grad_rows, 0, 0).astype(BF16)
    grad_up = dot(second_rows, grad_upper, 0, 0).astype(BF16)
    grad_up_weight = lax.psum_scatter(grad_up, "dp", scatter_dimension=0, tiled=True).astype(F32)
    grad_down_weight = lax.psum_scatter(
        grad_down, "dp", scatter_dimension=1, tiled=True
    ).astype(F32)

    grad_out = cotangent.astype(F32)
    grad_from_norm, gain_two, shift_two = norm_backward(
        grad_second, scaled_two, inverse_two, norm_gain[1]
    )
    grad_middle = grad_out + grad_from_norm
    grad_attn = grad_middle.astype(BF16)
    mixed_grads = dot(out_full, grad_attn, 1, 1).astype(BF16)
    grads_t = jnp.concatenate(exchange_blocks(rows_of(mixed_grads, tensor_size)), axis=1)
    out_partial = dot(mixed_all, grad_attn, 1, 0).astype(BF16)
    grad_out_mine = scatter_blocks(rows_of(out_partial, tensor_size)).astype(BF16)
    grad_out_weight = lax.psum_scatter(
        grad_out_mine, "dp", scatter_dimension=1, tiled=True
    ).astype(F32)

    early = jnp.stack(
        [gain_two, shift_two, jnp.sum(grad_middle, axis=0), jnp.sum(grad_out, axis=0)]
    )
    early = sum_over(early, ("dp", "tensor"))
    grad_up_bias = sum_over(grad_up_bias.reshape(-1, 128), ("dp",)).reshape(-1)

    query_low, key_low, value_low = attend_backward(
        place, slopes, queries_t, keys, values, grads_t, mixed_full, logs, local_rows, head_dim
    )
    normed_partial = (
        dot(query_low, qkv_full[0], 0, 1)
        + dot(key_low, qkv_full[1], 1, 1)
        + dot(value_low, qkv_full[2], 1, 1)
    ).astype(BF16)
    grad_normed = scatter_blocks(rows_of(normed_partial, tensor_size))
    grad_qkv_local = jnp.stack(
        [
            dot(normed_rows, query_low, 0, 1),
            dot(normed_rows, key_low, 0, 0),
            dot(normed_rows, value_low, 0, 0),
        ]
    ).astype(BF16)
    grad_qkv = lax.psum_scatter(grad_qkv_local, "dp", scatter_dimension=1, tiled=True).astype(F32)
    grad_from_first, gain_one, shift_one = norm_backward(
        grad_normed, scaled_one, inverse_one, norm_gain[0]
    )
    grad_in = grad_middle + grad_from_first
    late = sum_over(jnp.stack([gain_one, shift_one]), ("dp", "tensor"))
    grad_qv = jnp.stack(
        [jnp.sum(query_low.astype(F32), axis=1), jnp.sum(value_low.astype(F32), axis=0)]
    )
    grad_qv_bias = sum_over(grad_qv, ("dp",))
    return (
        block_out,
        grad_in,
        jnp.stack([late[0], early[0]]),
        jnp.stack([late[1], early[1]]),
        grad_qkv,
        grad_qv_bias,
        grad_out_weight,
        early[2:4],
        grad_up_weight,
        grad_up_bias,
        grad_down_weight,
    )


def solution(mesh):
    return jax.shard_map(
        body,
        mesh=mesh,
        in_specs=(
            P(("dp", "tensor"), None),
            P(),
            P(),
            P(None, "dp", "tensor"),
            P(None, "tensor"),
            P("tensor", "dp"),
            P(),
            P("dp", "tensor"),
            P("tensor"),
            P("tensor", "dp"),
            P(("dp", "tensor"), None),
        ),
        out_specs=(
            P(("dp", "tensor"), None),
            P(("dp", "tensor"), None),
            P(),
            P(),
            P(None, "dp", "tensor"),
            P(None, "tensor"),
            P("tensor", "dp"),
            P(),
            P("dp", "tensor"),
            P("tensor"),
            P("tensor", "dp"),
        ),
        check_vma=False,
    )
```

```python
import functools
import math

import jax
import jax.numpy as jnp
from jax import lax
from jax.experimental import pallas as pl
from jax.experimental.pallas import tpu as pltpu
from jax.sharding import PartitionSpec as P

HEADS = 16
LOG2E = 1.4426950408889634
NEG = -1e30
BF16 = jnp.bfloat16
F32 = jnp.float32


def normalise(values):
    average = jnp.mean(values, axis=-1, keepdims=True)
    centered = values - average
    inverse = lax.rsqrt(jnp.mean(centered * centered, axis=-1, keepdims=True) + 1e-05)
    return centered * inverse, inverse


def gelu_both(values):
    first = 0.7978845608
    square = values * values
    tangent = jnp.tanh(values * (first + (first * 0.044715) * square))
    half = 0.5 + 0.5 * tangent
    active = values * half
    slope = half + (values - values * (tangent * tangent)) * (
        0.5 * first + (1.5 * 0.044715 * first) * square
    )
    return active, slope


def first_norm_kernel(hidden, gain, shift, put_normed):
    scaled, _ = normalise(hidden().astype(F32))
    put_normed((scaled * gain()[0:1, :] + shift()[0:1, :]).astype(BF16))


def second_norm_kernel(hidden, attn, bias, gain, shift, put_middle, put_normed):
    middle = hidden().astype(F32) + attn() + bias()[0:1, :]
    put_middle(middle)
    scaled, _ = normalise(middle)
    put_normed((scaled * gain()[1:2, :] + shift()[1:2, :]).astype(BF16))


def back_of_norm(value, own, near, far, gain):
    scaled, inverse = normalise(value.astype(F32))
    gradient = own.astype(F32) + near.astype(F32) + far.astype(F32)
    grad_scaled = gradient * gain
    grad_mean = jnp.mean(grad_scaled, axis=-1, keepdims=True)
    grad_proj = jnp.mean(grad_scaled * scaled, axis=-1, keepdims=True)
    return inverse * (grad_scaled - grad_mean - scaled * grad_proj), gradient, scaled


def second_back_kernel(middle, above, own, near, far, gain, put_total, put_low, add_sums):
    change, gradient, scaled = back_of_norm(middle(), own(), near(), far(), gain()[1:2, :])
    grads = above().astype(F32)
    total = grads + change
    put_total(total)
    put_low(total.astype(BF16))
    columns = [gradient * scaled, gradient, total, grads]
    add_sums(jnp.concatenate([jnp.sum(c, axis=0, keepdims=True) for c in columns], axis=0))


def first_back_kernel(hidden, above, own, near, far, gain, put_total):
    change, _, _ = back_of_norm(hidden(), own(), near(), far(), gain()[0:1, :])
    put_total(above() + change)


def row_call(kernel, rows, width, arrays, outs, name, tile=128):
    tile = min(tile, rows // 2)
    half = rows // 2 // tile

    def specs(array):
        if isinstance(array, tuple):
            return [
                pl.BlockSpec((tile, width), lambda i: (jnp.minimum(i, half - 1), 0)),
                pl.BlockSpec((tile, width), lambda i: (jnp.maximum(i - half, 0), 0)),
            ]
        if array.shape[0] == rows:
            return [pl.BlockSpec((tile, width), lambda i: (i, 0))]
        return [pl.BlockSpec(array.shape, lambda i: (0, 0))]

    def flat(values):
        return [v for value in values for v in (value if isinstance(value, tuple) else (value,))]

    def run(*refs):
        step = pl.program_id(0)
        at = 0
        accesses = []
        for k, value in enumerate(arrays + outs):
            reads = k < len(arrays)
            if isinstance(value, tuple):
                one, two = refs[at : at + 2]
                at += 2
                if reads:
                    accesses.append(lambda a=one, b=two: jnp.where(step < half, a[...], b[...]))
                else:

                    def put(block, a=one, b=two):
                        @pl.when(step < half)
                        def _():
                            a[...] = block

                        @pl.when(step >= half)
                        def _():
                            b[...] = block

                    accesses.append(put)
                continue
            ref = refs[at]
            at += 1
            if reads:
                accesses.append(lambda a=ref: a[...])
            elif value.shape[0] == rows:

                def put(block, a=ref):
                    a[...] = block

                accesses.append(put)
            else:

                def add(block, a=ref):
                    @pl.when(step == 0)
                    def _():
                        a[...] = block

                    @pl.when(step > 0)
                    def _():
                        a[...] += block

                accesses.append(add)
        kernel(*accesses)

    results = pl.pallas_call(
        run,
        grid=(2 * half,),
        in_specs=[spec for a in arrays for spec in specs(a)],
        out_specs=[spec for o in outs for spec in specs(o)],
        out_shape=flat(outs),
        compiler_params=pltpu.CompilerParams(vmem_limit_bytes=32 * 2**20),
        cost_estimate=pl.CostEstimate(
            flops=20 * rows * width, bytes_accessed=12 * rows * width, transcendentals=rows
        ),
        name=name,
    )(*flat(arrays))
    results = list(results)
    return [
        (results.pop(0), results.pop(0)) if isinstance(o, tuple) else results.pop(0) for o in outs
    ]


def feed_kernel(count, *refs):
    seconds, grads = refs[:count], refs[count : 2 * count]
    up_ref, down_ref, bias_ref, before_ref = refs[2 * count : 2 * count + 4]
    mlps, backs = refs[2 * count + 4 : 3 * count + 4], refs[3 * count + 4 : 4 * count + 4]
    active_ref, upper_ref, sums_ref, second_ref, grad_ref, mlp_ref, back_ref = refs[4 * count + 4 :]
    step = pl.program_id(0)
    for k in range(count):

        @pl.when(step == k)
        def _(k=k):
            second_ref[...] = seconds[k][...]
            grad_ref[...] = grads[k][...]

    contract = (((1,), (1,)), ((), ()))
    upper = jnp.dot(second_ref[...], up_ref[...], preferred_element_type=F32) + bias_ref[...]
    active, slope = gelu_both(upper)
    active = active.astype(BF16)
    active_ref[...] = active
    grad_active = jnp.dot(grad_ref[...], down_ref[...], preferred_element_type=F32)
    grad_upper = (grad_active * slope).astype(BF16)
    upper_ref[...] = grad_upper
    back_ref[...] = lax.dot_general(
        grad_upper, up_ref[...], contract, preferred_element_type=F32
    ).astype(BF16)
    mlp_ref[...] = lax.dot_general(
        active, down_ref[...], contract, preferred_element_type=F32
    ).astype(BF16)
    for k in range(count):

        @pl.when(step == k)
        def _(k=k):
            mlps[k][...] = mlp_ref[...]
            backs[k][...] = back_ref[...]

    @pl.when(step == 0)
    def _():
        sums_ref[...] = before_ref[...]

    sums_ref[...] += jnp.sum(grad_upper.astype(F32), axis=0, keepdims=True)


def feed(tile, seconds, grads, weights, bias, before, name):
    count = len(seconds)
    width = seconds[0][0].shape[1]
    hidden = bias.shape[1]
    block = pl.BlockSpec((tile, width), lambda i: (0, 0))

    def at(k):
        return pl.BlockSpec((tile, width), lambda i: (k, 0))

    by_hidden = pl.BlockSpec((tile, hidden), lambda i: (i, 0))
    row = pl.BlockSpec((1, hidden), lambda i: (0, 0))
    results = pl.pallas_call(
        functools.partial(feed_kernel, count),
        grid=(count,),
        in_specs=[at(k) for _, k in seconds + grads]
        + [
            pl.BlockSpec((width, hidden), lambda i: (0, 0)),
            pl.BlockSpec((width, hidden), lambda i: (0, 1)),
            row,
            row,
        ],
        out_specs=[block] * (2 * count) + [by_hidden, by_hidden, row],
        out_shape=[jax.ShapeDtypeStruct((tile, width), BF16)] * (2 * count)
        + [
            jax.ShapeDtypeStruct((count * tile, hidden), BF16),
            jax.ShapeDtypeStruct((count * tile, hidden), BF16),
            jax.ShapeDtypeStruct((1, hidden), F32),
        ],
        scratch_shapes=[pltpu.VMEM((tile, width), BF16)] * 4,
        compiler_params=pltpu.CompilerParams(vmem_limit_bytes=50 * 2**20),
        cost_estimate=pl.CostEstimate(
            flops=8 * count * tile * width * hidden,
            bytes_accessed=16 * 2**20,
            transcendentals=count * tile * hidden,
        ),
        name=name,
    )(*(a for a, _ in seconds + grads), weights, weights, bias, before)
    return results[:count], results[count : 2 * count], results[-3], results[-2], results[-1]


def weight_kernel(blocks, groups, *refs):
    out_ref = refs[-1]
    rights = refs[2 * blocks : -1]
    hidden = rights[0].shape[1]
    for side in range(2):
        lefts = refs[side * blocks : (side + 1) * blocks]
        total = None
        at = 0
        for g, count in enumerate(groups):
            left = jnp.concatenate([lefts[at + k][...] for k in range(count)], axis=0)
            at += count
            term = lax.dot_general(
                left,
                rights[side * len(groups) + g][...],
                (((0,), (0,)), ((), ())),
                preferred_element_type=F32,
            )
            total = term if total is None else total + term
        out_ref[:, side * hidden : (side + 1) * hidden] = total.astype(BF16)


def weight_grads(rows, seconds, grads, uppers, actives):
    groups = [len(g) for g in seconds]
    lefts = [b for g in seconds for b in g] + [b for g in grads for b in g]
    blocks = sum(groups)
    width = lefts[0][0].shape[1]
    hidden = uppers[0].shape[1]
    tile = min(256, width)

    def at(k):
        return pl.BlockSpec((rows, tile), lambda i: (k, i))

    return pl.pallas_call(
        functools.partial(weight_kernel, blocks, groups),
        grid=(width // tile,),
        in_specs=[at(k) for _, k in lefts]
        + [pl.BlockSpec(r.shape, lambda i: (0, 0)) for r in uppers + actives],
        out_specs=pl.BlockSpec((tile, 2 * hidden), lambda i: (i, 0)),
        out_shape=jax.ShapeDtypeStruct((width, 2 * hidden), BF16),
        compiler_params=pltpu.CompilerParams(vmem_limit_bytes=50 * 2**20),
        cost_estimate=pl.CostEstimate(
            flops=4 * blocks * rows * width * hidden, bytes_accessed=20 * 2**20, transcendentals=0
        ),
        name="weight_grads",
    )(*(a for a, _ in lefts), *uppers, *actives)


def fill_bias(bias, masked, slope):
    size = bias.shape[0]
    key = lax.broadcasted_iota(jnp.int32, (size, size), 0)
    query = lax.broadcasted_iota(jnp.int32, (size, size), 1)
    value = key.astype(F32) * slope
    bias[...] = value
    masked[...] = jnp.where(key <= query, value, NEG)


def head_rows(block, head):
    half = block.shape[0] // 2
    rows = lax.broadcasted_iota(jnp.int32, block.shape, 0)
    keep = (rows < half) if head == 0 else (rows >= half)
    return jnp.where(keep, block, jnp.zeros_like(block))


def forward_kernel(
    place, slope_ref, q_ref, k_ref, v_ref, mixed_ref, full_ref, log_ref, bias, masked, values_t, *, scale, pair
):
    query_block = pl.program_id(0)
    me = place[0]
    size = bias.shape[1]
    half = q_ref.shape[0] // 2

    @pl.when(query_block == 0)
    def _():
        values_t[...] = v_ref[...].T
        for head in range(2):
            fill_bias(bias.at[head], masked.at[head], slope_ref[2 * pair + head])

    outputs = []
    logs = []
    for head in range(2):
        step = slope_ref[2 * pair + head] * size
        queries = head_rows(q_ref[...], head)

        def block(key_block, carry, bias_block, head=head, step=step, queries=queries):
            top, total, acc = carry
            at = pl.multiple_of((key_block ^ me) * size, size)
            raw = jnp.dot(k_ref[pl.ds(at, size), :], queries, preferred_element_type=F32)
            scores = raw * scale + bias_block
            base = key_block.astype(F32) * step
            new_top = jnp.maximum(top, jnp.max(scores, axis=0, keepdims=True) + base)
            weights = jnp.exp2(scores - (new_top - base))
            fade = jnp.exp2(top - new_top)
            total = total * fade + jnp.sum(weights, axis=0, keepdims=True)
            rows = values_t[head * half : (head + 1) * half, pl.ds(at, size)]
            acc = acc * fade + jnp.dot(rows, weights.astype(BF16), preferred_element_type=F32)
            return new_top, total, acc

        start = (
            jnp.full((1, size), NEG, F32),
            jnp.zeros((1, size), F32),
            jnp.zeros((half, size), F32),
        )
        carry = lax.fori_loop(
            0, query_block, lambda i, c, head=head, block=block: block(i, c, bias[head]), start
        )
        top, total, acc = block(query_block, carry, masked[head])
        outputs.append(acc / total)
        logs.append(top + jnp.log2(total))
    result = jnp.concatenate(outputs, axis=0)
    full_ref[...] = result
    mixed_ref[...] = result.astype(BF16)
    log_ref[...] = jnp.concatenate(logs, axis=0)


def backward_kernel(
    place,
    slope_ref,
    q_ref,
    k_ref,
    v_ref,
    g_ref,
    full_ref,
    log_ref,
    gq_ref,
    gk_ref,
    gv_ref,
    sums_ref,
    bias,
    masked,
    gq_acc,
    delta,
    *,
    scale,
    factor,
    pair,
):
    key_block = pl.program_id(0)
    blocks = pl.num_programs(0)
    me = place[0]
    size = bias.shape[1]
    half = q_ref.shape[0] // 2

    @pl.when(key_block == 0)
    def _():
        gq_acc[...] = jnp.zeros_like(gq_acc)
        for head in range(2):
            fill_bias(bias.at[head], masked.at[head], slope_ref[2 * pair + head])
            rows = slice(head * half, (head + 1) * half)
            delta[head : head + 1, :] = jnp.sum(
                g_ref[rows, :].astype(F32) * full_ref[rows, :], axis=0, keepdims=True
            )

    keys = k_ref[...]
    keys_t = keys.T
    values = v_ref[...]
    grad_k = jnp.zeros(keys.shape, F32)
    grad_v = jnp.zeros(keys.shape, F32)
    for head in range(2):
        base = key_block.astype(F32) * (slope_ref[2 * pair + head] * size)
        rows = slice(head * half, (head + 1) * half)

        def block(query_block, carry, bias_block, head=head, base=base, rows=rows):
            grad_k, grad_v = carry
            at = pl.multiple_of((query_block ^ me) * size, size)
            queries = head_rows(q_ref[:, pl.ds(at, size)], head)
            grads = head_rows(g_ref[:, pl.ds(at, size)], head)
            raw = jnp.dot(keys, queries, preferred_element_type=F32)
            log = log_ref[head : head + 1, pl.ds(at, size)] - base
            weights = jnp.exp2(raw * scale + (bias_block - log))
            along = jnp.dot(values, grads, preferred_element_type=F32)
            change = (weights * (along - delta[head : head + 1, pl.ds(at, size)])).astype(BF16)
            contract = (((1,), (1,)), ((), ()))
            grad_v = grad_v + lax.dot_general(
                weights.astype(BF16), grads, contract, preferred_element_type=F32
            )
            grad_k = grad_k + lax.dot_general(change, queries, contract, preferred_element_type=F32)
            gq_acc[rows, pl.ds(at, size)] += jnp.dot(
                keys_t[rows, :], change, preferred_element_type=F32
            )
            return grad_k, grad_v

        carry = block(key_block, (grad_k, grad_v), masked[head])
        grad_k, grad_v = lax.fori_loop(
            key_block + 1, blocks, lambda i, c, head=head, block=block: block(i, c, bias[head]), carry
        )
    low_k = (grad_k * factor).astype(BF16)
    low_v = grad_v.astype(BF16)
    gk_ref[...] = low_k
    gv_ref[...] = low_v
    sums = jnp.concatenate(
        [jnp.sum(low.astype(F32), axis=0, keepdims=True) for low in (low_k, low_v)], axis=0
    )

    @pl.when(key_block == 0)
    def _():
        sums_ref[...] = sums

    @pl.when(key_block > 0)
    def _():
        sums_ref[...] += sums

    @pl.when(key_block == blocks - 1)
    def _():
        gq_ref[...] = (gq_acc[...] * factor).astype(BF16)


def attend_forward(place, slopes, queries_t, keys, values, size, head_dim, pair):
    length = queries_t.shape[1]
    wide = 2 * head_dim
    along_q = pl.BlockSpec((wide, size), lambda i, me, s: (pair, i ^ me[0]))
    out_q = pl.BlockSpec((wide, size), lambda i, me, s: (0, i ^ me[0]))
    whole = pl.BlockSpec((length, wide), lambda i, me, s: (0, pair))
    return pl.pallas_call(
        functools.partial(forward_kernel, scale=LOG2E / math.sqrt(head_dim), pair=pair),
        grid_spec=pltpu.PrefetchScalarGridSpec(
            num_scalar_prefetch=2,
            grid=(length // size,),
            in_specs=[along_q, whole, whole],
            out_specs=[out_q, out_q, pl.BlockSpec((2, size), lambda i, me, s: (0, i ^ me[0]))],
            scratch_shapes=[
                pltpu.VMEM((2, size, size), F32),
                pltpu.VMEM((2, size, size), F32),
                pltpu.VMEM((wide, length), BF16),
            ],
        ),
        out_shape=[
            jax.ShapeDtypeStruct((wide, length), BF16),
            jax.ShapeDtypeStruct((wide, length), F32),
            jax.ShapeDtypeStruct((2, length), F32),
        ],
        compiler_params=pltpu.CompilerParams(vmem_limit_bytes=48 * 2**20),
        cost_estimate=pl.CostEstimate(
            flops=10 * 10**9, bytes_accessed=4 * 2**20, transcendentals=5 * 10**6
        ),
        name=f"attend_forward_{pair}",
    )(place, slopes, queries_t, keys, values)


def attend_backward(place, slopes, queries_t, keys, values, grads_t, full, logs, size, head_dim, pair):
    length = queries_t.shape[1]
    wide = 2 * head_dim
    along_k = pl.BlockSpec((size, wide), lambda i, me, s: (i ^ me[0], pair))
    out_k = pl.BlockSpec((size, wide), lambda i, me, s: (i ^ me[0], 0))
    all_q = pl.BlockSpec((wide, length), lambda i, me, s: (pair, 0))
    whole = pl.BlockSpec((wide, length), lambda i, me, s: (0, 0))
    return pl.pallas_call(
        functools.partial(
            backward_kernel,
            scale=LOG2E / math.sqrt(head_dim),
            factor=1.0 / math.sqrt(head_dim),
            pair=pair,
        ),
        grid_spec=pltpu.PrefetchScalarGridSpec(
            num_scalar_prefetch=2,
            grid=(length // size,),
            in_specs=[
                all_q,
                along_k,
                along_k,
                whole,
                whole,
                pl.BlockSpec((2, length), lambda i, me, s: (0, 0)),
            ],
            out_specs=[whole, out_k, out_k, pl.BlockSpec((2, wide), lambda i, me, s: (0, 0))],
            scratch_shapes=[
                pltpu.VMEM((2, size, size), F32),
                pltpu.VMEM((2, size, size), F32),
                pltpu.VMEM((wide, length), F32),
                pltpu.VMEM((2, length), F32),
            ],
        ),
        out_shape=[
            jax.ShapeDtypeStruct((wide, length), BF16),
            jax.ShapeDtypeStruct((length, wide), BF16),
            jax.ShapeDtypeStruct((length, wide), BF16),
            jax.ShapeDtypeStruct((2, wide), F32),
        ],
        compiler_params=pltpu.CompilerParams(vmem_limit_bytes=48 * 2**20),
        cost_estimate=pl.CostEstimate(
            flops=20 * 10**9, bytes_accessed=6 * 2**20, transcendentals=5 * 10**6
        ),
        name=f"attend_backward_{pair}",
    )(place, slopes, queries_t, keys, values, grads_t, full, logs)


def swap(value, axis, distance):
    size = lax.axis_size(axis)
    return lax.ppermute(value, axis, [(i, i ^ distance) for i in range(size)])


def after(value, *earlier):
    return lax.optimization_barrier((value,) + earlier)[0]


def exchange_blocks(parts):
    return [parts[0]] + [swap(parts[j], "tensor", j) for j in range(1, 4)]


def chip_sum(far, far_near):
    return (far.astype(F32) + swap(far_near, "tensor", 1).astype(F32)).astype(BF16)


def sum_over(value, axes):
    for axis in axes:
        size = lax.axis_size(axis)
        distance = 1
        while distance < size:
            if distance * 4 <= size:
                one, two, three = (swap(value, axis, distance * k) for k in (1, 2, 3))
                value = (value + one) + (two + three)
                distance *= 4
            else:
                value = value + swap(value, axis, distance)
                distance *= 2
    return value


def gather_dp(shard):
    count = lax.axis_size("dp")
    me = lax.axis_index("dp")
    rows = shard.shape[0]
    blocks = [(0, shard)]
    distance = count // 2
    while distance > 1:
        blocks = blocks + [(o + distance, swap(block, "dp", distance)) for o, block in blocks]
        distance //= 2
    whole = jnp.zeros((count * rows, shard.shape[1]), shard.dtype)
    for offset, block in blocks:
        for o, piece in ((offset, block), (offset + 1, swap(block, "dp", 1))):
            whole = lax.dynamic_update_slice(whole, piece, ((me ^ o) * rows, 0))
    return whole, [block for _, block in blocks[1:]]


def scatter_dp_parts(whole):
    count = lax.axis_size("dp")
    me = lax.axis_index("dp")
    rows, width = whole.shape[0] // count, whole.shape[1]

    def blocks(start):
        return jnp.concatenate(
            [
                lax.dynamic_slice(whole, ((me ^ d) * rows, 0), (rows, width))
                for d in range(start, count, 2)
            ],
            axis=0,
        )

    return blocks(0), blocks(1)


def scatter_dp_last(even):
    parts = rows_of(even, lax.axis_size("dp") // 2)
    total = parts[0].astype(F32)
    for k, part in enumerate(parts[1:]):
        total = total + swap(part, "dp", 2 * k + 2).astype(F32)
    return total


def rows_of(value, count):
    size = value.shape[0] // count
    return [value[i * size : (i + 1) * size] for i in range(count)]


def dot(a, b, ca, cb):
    return lax.dot_general(a, b, (((ca,), (cb,)), ((), ())), preferred_element_type=F32)


def body(
    hidden_in,
    norm_gain,
    norm_shift,
    qkv_weight,
    qv_bias,
    out_weight,
    out_bias,
    up_weight,
    up_bias,
    down_weight,
    cotangent,
):
    rows, width = hidden_in.shape
    tensor_size = lax.axis_size("tensor")
    heads_wide = qkv_weight.shape[2]
    hidden_units = up_weight.shape[1]
    local_heads = HEADS // tensor_size
    head_dim = heads_wide // local_heads
    pairs = local_heads // 2
    wide = 2 * head_dim
    me = lax.axis_index("tensor").astype(jnp.int32)
    place = me.reshape(1)
    head_ids = me * local_heads + jnp.arange(local_heads, dtype=jnp.int32)
    slopes = jnp.exp2(-8.0 * (head_ids.astype(F32) + 1.0) / HEADS) * LOG2E
    part = rows // 2
    stat = functools.partial(row_call, rows=rows, width=width)
    row_f32 = jax.ShapeDtypeStruct((rows, width), F32)
    row_bf16 = jax.ShapeDtypeStruct((rows, width), BF16)
    part_bf16 = jax.ShapeDtypeStruct((part, width), BF16)
    four_f32 = jax.ShapeDtypeStruct((4, width), F32)

    first_shard = jnp.concatenate(
        [qkv_weight[0], qkv_weight[1], qkv_weight[2], out_weight.T], axis=1
    )
    second_shard = jnp.concatenate([up_weight, down_weight.T], axis=1)
    first_full, first_others = gather_dp(first_shard)
    second_full = lax.all_gather(after(second_shard, *first_others), "dp", axis=0, tiled=True)

    (normed,) = stat(
        first_norm_kernel, arrays=[hidden_in, norm_gain, norm_shift], outs=[row_bf16], name="norm_one"
    )
    normed_far = after(swap(normed, "tensor", 2), *first_others)
    normed_near = swap(normed, "tensor", 1)
    normed_rows = jnp.concatenate(
        [normed, normed_near, normed_far, swap(normed_far, "tensor", 1)], axis=0
    )
    grads_far = swap(cotangent, "tensor", 2)
    normed_rows = after(normed_rows, grads_far)
    grads_near = swap(cotangent, "tensor", 1)
    grads_far_near = swap(grads_far, "tensor", 1)

    w_query, w_key, w_value = (
        first_full[:, c * heads_wide : (c + 1) * heads_wide] for c in range(3)
    )
    queries_t = (dot(w_query, normed_rows, 0, 1) + qv_bias[0][:, None]).astype(BF16)
    keys = dot(normed_rows, w_key, 1, 0).astype(BF16)
    values = (dot(normed_rows, w_value, 1, 0) + qv_bias[1]).astype(BF16)
    out_mine = first_full[:, 3 * heads_wide :]
    out_far = swap(out_mine, "tensor", 2)
    kept = []
    mixed_parts = [[] for _ in range(tensor_size)]
    received = out_far
    for pair in range(pairs):
        mixed_t, mixed_full, logs = attend_forward(
            place,
            slopes,
            queries_t if pair == 0 else after(queries_t, out_far, mixed_full),
            keys,
            values,
            rows,
            head_dim,
            pair,
        )
        if pair > 0:
            mixed_t = after(mixed_t, *received)
        kept.append((mixed_full, logs))
        parts = [mixed_t[:, j * rows : (j + 1) * rows] for j in range(tensor_size)]
        received = exchange_blocks(parts)
        for j, block in enumerate(received):
            mixed_parts[j].append(block)
    out_full = jnp.concatenate(
        [out_mine, swap(out_mine, "tensor", 1), out_far, swap(out_far, "tensor", 1)], axis=1
    )
    mixed_all = jnp.concatenate([block for group in mixed_parts for block in group], axis=0)
    attn_sum = dot(mixed_all, out_full, 0, 1)
    middle, second = stat(
        second_norm_kernel,
        arrays=[hidden_in, attn_sum, out_bias, norm_gain, norm_shift],
        outs=[row_f32, (part_bf16, part_bf16)],
        name="norm_two",
    )

    up_bias_row = up_bias.reshape(1, hidden_units)
    far_chunks = [swap(second[c], "tensor", 2) for c in range(2)]
    seconds = [[(block, 0) for block in second]]
    seconds[0] += [(swap(block, "tensor", 1), 0) for block in second]
    grads = [[(g, c) for g in (cotangent, grads_near) for c in range(2)]]
    mlp_a, back_a, active, upper, sums_up = feed(
        part, seconds[0], grads[0], second_full, up_bias_row, jnp.zeros_like(up_bias_row), "feed_near"
    )
    actives, uppers = [active], [upper]
    mlps, back_fars = [], []
    earlier = (mlp_a[0],)
    for c in range(2):
        far = after(far_chunks[c], *earlier)
        pair_c = [(far, 0), (swap(far, "tensor", 1), 0)]
        if c > 0:
            pair_c[0] = (after(far, mine), 0)
        grads_c = [(grads_far, c), (grads_far_near, c)]
        mlp_c, back_c, active, upper, sums_up = feed(
            part, pair_c, grads_c, second_full, up_bias_row, sums_up, f"feed_far_{c}"
        )
        earlier = (mlp_c[0],)
        seconds.append(pair_c)
        grads.append(grads_c)
        actives.append(active)
        uppers.append(upper)
        mlps.append(mlp_c)
        mine = chip_sum(back_c[0], after(back_c[1], *back_fars))
        back_fars.append(swap(mine, "tensor", 2))
    back_near = tuple(swap(back_a[2 + c], "tensor", 1) for c in range(2))

    uppers[0] = after(uppers[0], back_fars[0], mine)
    grad_second_w = weight_grads(part, seconds, grads, uppers, actives)
    grad_second_w = lax.psum_scatter(
        grad_second_w, "dp", scatter_dimension=0, tiled=True
    ).astype(F32)
    grad_up_weight = grad_second_w[:, :hidden_units]
    grad_down_weight = grad_second_w[:, hidden_units:].T

    grad_middle, grad_attn, early = stat(
        second_back_kernel,
        arrays=[middle, cotangent, tuple(back_a[:2]), back_near, tuple(back_fars), norm_gain],
        outs=[row_f32, row_bf16, four_f32],
        name="norm_two_back",
    )
    mixed_grads = dot(out_full, grad_attn, 0, 1).astype(BF16)
    mlps = [lax.optimization_barrier((*m, grad_attn))[:2] for m in mlps]
    mlp_a = lax.optimization_barrier((*mlp_a, grad_attn))[:4]
    grads_t = []
    for pair in range(pairs):
        parts = [
            mixed_grads[j * heads_wide + pair * wide : j * heads_wide + (pair + 1) * wide]
            for j in range(tensor_size)
        ]
        grads_t.append(jnp.concatenate(exchange_blocks(parts), axis=1))

    out_partial = dot(after(grad_attn, mixed_grads), mixed_all, 0, 1).astype(BF16)
    out_cols = [out_partial[:, j * heads_wide : (j + 1) * heads_wide] for j in range(tensor_size)]
    out_mine_sum = chip_sum(out_cols[2], out_cols[3])
    out_far_sum = swap(out_mine_sum, "tensor", 2)
    mlp_mine_sum = jnp.concatenate([chip_sum(m[0], m[1]) for m in mlps], axis=0)
    mlp_far = swap(after(mlp_mine_sum, out_far_sum), "tensor", 2)
    mlp_near = swap(jnp.concatenate(mlp_a[2:], axis=0), "tensor", 1)
    mlp_own = jnp.concatenate(mlp_a[:2], axis=0)
    block_out = (
        middle
        + (mlp_own.astype(F32) + mlp_near.astype(F32) + mlp_far.astype(F32))
        + out_bias[1]
    )
    low = []
    first_sums = []
    for pair in range(pairs):
        grads_pair = grads_t[pair]
        if pair == 0:
            grads_pair = after(grads_pair, out_mine_sum, mlp_mine_sum)
        else:
            grads_pair = after(grads_pair, low[-1][0], out_far_sum)
        mixed_full, logs = kept[pair]
        low.append(
            attend_backward(
                place, slopes, queries_t, keys, values, grads_pair, mixed_full, logs, rows, head_dim, pair
            )
        )
    sent = []
    piece_groups = []
    for pair in range(pairs):
        if pair == pairs - 1 and pair > 0:
            held = lax.optimization_barrier((*low[pair], mlp_far, *(x[1] for x in sent)))
            low[pair] = held[:4]
            sent = [(x[0], arrived) for x, arrived in zip(sent, held[5:])]
        query_p, key_p, value_p, _ = low[pair]
        pieces = [
            dot(normed_rows, query_p, 0, 1).astype(BF16),
            dot(normed_rows, key_p, 0, 0).astype(BF16),
            dot(normed_rows, value_p, 0, 0).astype(BF16),
        ]
        piece_groups.append(list(pieces))
        if pair == pairs - 1:
            pieces.append(
                (
                    out_cols[0].astype(F32)
                    + swap(out_cols[1], "tensor", 1).astype(F32)
                    + out_far_sum.astype(F32)
                ).astype(BF16)
            )
        keep, send = scatter_dp_parts(jnp.concatenate(pieces, axis=1))
        sent.append((keep, swap(send, "dp", 1)))

    query_low = after(jnp.concatenate([g[0] for g in low], axis=0), send)
    key_low = jnp.concatenate([g[1] for g in low], axis=1)
    value_low = jnp.concatenate([g[2] for g in low], axis=1)

    def normed_grads(at, query_low):
        return (
            dot(query_low[:, at], w_query, 0, 1)
            + dot(key_low[at], w_key, 1, 1)
            + dot(value_low[at], w_value, 1, 1)
        ).astype(BF16)

    half = 2 * rows
    far_grads = normed_grads(slice(half, 2 * half), query_low)
    first_mine = chip_sum(far_grads[:rows], far_grads[rows:])
    first_far = swap(first_mine, "tensor", 2)
    near_grads = normed_grads(slice(0, half), after(query_low, first_mine))
    first_near = swap(near_grads[rows:], "tensor", 1)

    for keep, arrived in sent:
        arrived = after(arrived, first_mine)
        first_sums.append((keep.astype(F32) + arrived.astype(F32)).astype(BF16))

    query_sums, value_sums = [], []
    gain_sum, shift_sum = 0.0, 0.0
    for pair in range(pairs):
        sums_p = after(low[pair][3], first_mine)
        query_sums.append(jnp.sum(after(low[pair][0], first_mine).astype(F32), axis=1))
        value_sums.append(sums_p[1])
        column_sums = (query_sums[-1], sums_p[0], sums_p[1])
        for weight, piece, column in zip(
            (w_query, w_key, w_value), piece_groups[pair], column_sums
        ):
            weight_p = weight[:, pair * wide : (pair + 1) * wide].astype(F32)
            gain_sum = gain_sum + jnp.sum(weight_p * after(piece, first_mine).astype(F32), axis=1)
            shift_sum = shift_sum + jnp.sum(weight_p * column[None, :], axis=1)
    gain_sum = (gain_sum - norm_shift[0] * shift_sum) / norm_gain[0]

    first_sums = scatter_dp_last(jnp.concatenate(first_sums, axis=1))
    grad_qkv = jnp.stack(
        [
            jnp.concatenate(
                [
                    first_sums[:, (3 * pair + c) * wide : (3 * pair + c + 1) * wide]
                    for pair in range(pairs)
                ],
                axis=1,
            )
            for c in range(3)
        ]
    )
    grad_out_weight = first_sums[:, 3 * heads_wide :].T

    (grad_in,) = stat(
        first_back_kernel,
        arrays=[hidden_in, grad_middle, near_grads[:rows], first_near, first_far, norm_gain],
        outs=[row_f32],
        name="norm_one_back",
    )
    lanes = 128
    whole_sums = jnp.concatenate([early, gain_sum[None], shift_sum[None]], axis=0).reshape(-1, lanes)
    split_sums = jnp.concatenate(query_sums + value_sums + [sums_up[0]]).reshape(-1, lanes)
    sums = sum_over(jnp.concatenate([whole_sums, split_sums], axis=0), ("dp",))
    whole_sums = sum_over(sums[: whole_sums.shape[0]], ("tensor",)).reshape(-1, width)
    split_sums = sums[whole_sums.size // lanes :].reshape(-1)
    return (
        block_out,
        grad_in,
        jnp.stack([whole_sums[4], whole_sums[0]]),
        jnp.stack([whole_sums[5], whole_sums[1]]),
        grad_qkv,
        split_sums[: 2 * heads_wide].reshape(2, heads_wide),
        grad_out_weight,
        whole_sums[2:4],
        grad_up_weight,
        split_sums[2 * heads_wide :],
        grad_down_weight,
    )


def solution(mesh):
    return jax.shard_map(
        body,
        mesh=mesh,
        in_specs=(
            P(("dp", "tensor"), None),
            P(),
            P(),
            P(None, "dp", "tensor"),
            P(None, "tensor"),
            P("tensor", "dp"),
            P(),
            P("dp", "tensor"),
            P("tensor"),
            P("tensor", "dp"),
            P(("dp", "tensor"), None),
        ),
        out_specs=(
            P(("dp", "tensor"), None),
            P(("dp", "tensor"), None),
            P(),
            P(),
            P(None, "dp", "tensor"),
            P(None, "tensor"),
            P("tensor", "dp"),
            P(),
            P("dp", "tensor"),
            P("tensor"),
            P("tensor", "dp"),
        ),
        check_vma=False,
    )
```

```python
import functools
import math

import jax
import jax.numpy as jnp
from jax import lax
from jax.experimental import pallas as pl
from jax.experimental.pallas import tpu as pltpu
from jax.sharding import PartitionSpec as P

HEADS = 16
LOG2E = 1.4426950408889634
NEG = -1e30
BF16 = jnp.bfloat16
F32 = jnp.float32


def normalise(values):
    average = jnp.mean(values, axis=-1, keepdims=True)
    centered = values - average
    inverse = lax.rsqrt(jnp.mean(centered * centered, axis=-1, keepdims=True) + 1e-05)
    return centered * inverse, inverse


def gelu_both(values):
    first = 0.7978845608
    square = values * values
    tangent = jnp.tanh(values * (first + (first * 0.044715) * square))
    half = 0.5 + 0.5 * tangent
    active = values * half
    slope = half + (values - values * (tangent * tangent)) * (
        0.5 * first + (1.5 * 0.044715 * first) * square
    )
    return active, slope


def first_norm_kernel(hidden, gain, shift, put_normed):
    scaled, _ = normalise(hidden().astype(F32))
    put_normed((scaled * gain()[0:1, :] + shift()[0:1, :]).astype(BF16))


def second_norm_kernel(hidden, attn, bias, gain, shift, put_middle, put_normed):
    middle = hidden().astype(F32) + attn() + bias()[0:1, :]
    put_middle(middle)
    scaled, _ = normalise(middle)
    put_normed((scaled * gain()[1:2, :] + shift()[1:2, :]).astype(BF16))


def back_of_norm(value, own, near, far, gain):
    scaled, inverse = normalise(value.astype(F32))
    gradient = own.astype(F32) + near.astype(F32) + far.astype(F32)
    grad_scaled = gradient * gain
    grad_mean = jnp.mean(grad_scaled, axis=-1, keepdims=True)
    grad_proj = jnp.mean(grad_scaled * scaled, axis=-1, keepdims=True)
    return inverse * (grad_scaled - grad_mean - scaled * grad_proj), gradient, scaled


def second_back_kernel(middle, above, own, near, far, gain, put_total, put_low, add_sums):
    change, gradient, scaled = back_of_norm(middle(), own(), near(), far(), gain()[1:2, :])
    grads = above().astype(F32)
    total = grads + change
    put_total(total)
    put_low(total.astype(BF16))
    columns = [gradient * scaled, gradient, total, grads]
    add_sums(jnp.concatenate([jnp.sum(c, axis=0, keepdims=True) for c in columns], axis=0))


def first_back_kernel(hidden, above, own, near, far, gain, put_total):
    change, _, _ = back_of_norm(hidden(), own(), near(), far(), gain()[0:1, :])
    put_total(above() + change)


def row_call(kernel, rows, width, arrays, outs, name, tile=128):
    tile = min(tile, rows // 2)
    half = rows // 2 // tile

    def specs(array):
        if isinstance(array, tuple):
            return [
                pl.BlockSpec((tile, width), lambda i: (jnp.minimum(i, half - 1), 0)),
                pl.BlockSpec((tile, width), lambda i: (jnp.maximum(i - half, 0), 0)),
            ]
        if array.shape[0] == rows:
            return [pl.BlockSpec((tile, width), lambda i: (i, 0))]
        return [pl.BlockSpec(array.shape, lambda i: (0, 0))]

    def flat(values):
        return [v for value in values for v in (value if isinstance(value, tuple) else (value,))]

    def run(*refs):
        step = pl.program_id(0)
        at = 0
        accesses = []
        for k, value in enumerate(arrays + outs):
            reads = k < len(arrays)
            if isinstance(value, tuple):
                one, two = refs[at : at + 2]
                at += 2
                if reads:
                    accesses.append(lambda a=one, b=two: jnp.where(step < half, a[...], b[...]))
                else:

                    def put(block, a=one, b=two):
                        @pl.when(step < half)
                        def _():
                            a[...] = block

                        @pl.when(step >= half)
                        def _():
                            b[...] = block

                    accesses.append(put)
                continue
            ref = refs[at]
            at += 1
            if reads:
                accesses.append(lambda a=ref: a[...])
            elif value.shape[0] == rows:

                def put(block, a=ref):
                    a[...] = block

                accesses.append(put)
            else:

                def add(block, a=ref):
                    @pl.when(step == 0)
                    def _():
                        a[...] = block

                    @pl.when(step > 0)
                    def _():
                        a[...] += block

                accesses.append(add)
        kernel(*accesses)

    results = pl.pallas_call(
        run,
        grid=(2 * half,),
        in_specs=[spec for a in arrays for spec in specs(a)],
        out_specs=[spec for o in outs for spec in specs(o)],
        out_shape=flat(outs),
        compiler_params=pltpu.CompilerParams(vmem_limit_bytes=32 * 2**20),
        cost_estimate=pl.CostEstimate(
            flops=20 * rows * width, bytes_accessed=12 * rows * width, transcendentals=rows
        ),
        name=name,
    )(*flat(arrays))
    results = list(results)
    return [
        (results.pop(0), results.pop(0)) if isinstance(o, tuple) else results.pop(0) for o in outs
    ]


def feed_kernel(count, ring, *refs):
    seconds, grads = refs[:count], refs[count : 2 * count]
    bias_ref, before_ref = refs[2 * count : 2 * count + 2]
    parts, refs = refs[2 * count + 2], refs[2 * count + 3 :]
    mlps, backs = refs[:count], refs[count : 2 * count]
    active_ref, upper_ref, sums_ref, weight_ref, arrived = refs[2 * count :]
    hidden = bias_ref.shape[1]
    up_ref, down_ref = weight_ref.at[:, :hidden], weight_ref.at[:, hidden:]
    step = pl.program_id(0)
    contract = (((1,), (1,)), ((), ()))

    @pl.when(step == 0)
    def _():
        sums_ref[...] = before_ref[...]
        rows = parts.shape[0] // len(ring)
        copies = [
            pltpu.make_async_copy(
                parts.at[at * rows : (at + 1) * rows, :],
                weight_ref.at[owner * rows : (owner + 1) * rows, :],
                arrived.at[at],
            )
            for at, owner in enumerate(ring)
        ]
        for copy in copies:
            copy.start()
        for copy in copies:
            copy.wait()

    for k in range(count):

        @pl.when(step == k)
        def _(k=k):
            upper = jnp.dot(seconds[k][...], up_ref[...], preferred_element_type=F32) + bias_ref[...]
            active, slope = gelu_both(upper)
            active = active.astype(BF16)
            active_ref[...] = active
            grad_active = jnp.dot(grads[k][...], down_ref[...], preferred_element_type=F32)
            grad_upper = (grad_active * slope).astype(BF16)
            upper_ref[...] = grad_upper
            backs[k][...] = lax.dot_general(
                grad_upper, up_ref[...], contract, preferred_element_type=F32
            ).astype(BF16)
            mlps[k][...] = lax.dot_general(
                active, down_ref[...], contract, preferred_element_type=F32
            ).astype(BF16)
            sums_ref[...] += jnp.sum(grad_upper.astype(F32), axis=0, keepdims=True)


def feed(tile, seconds, grads, weights, bias, before, name):
    count, ring = len(seconds), ring_dp()
    width = seconds[0][0].shape[1]
    hidden = bias.shape[1]
    block = pl.BlockSpec((tile, width), lambda i: (0, 0))

    def at(k):
        return pl.BlockSpec((tile, width), lambda i: (k, 0))

    by_hidden = pl.BlockSpec((tile, hidden), lambda i: (i, 0))
    row = pl.BlockSpec((1, hidden), lambda i: (0, 0))
    results = pl.pallas_call(
        functools.partial(feed_kernel, count, ring),
        grid=(count,),
        in_specs=[at(k) for _, k in seconds + grads]
        + [row, row, pl.BlockSpec(memory_space=pl.ANY)],
        out_specs=[block] * (2 * count) + [by_hidden, by_hidden, row],
        scratch_shapes=[
            pltpu.VMEM((width, 2 * hidden), BF16),
            pltpu.SemaphoreType.DMA((len(ring),)),
        ],
        out_shape=[jax.ShapeDtypeStruct((tile, width), BF16)] * (2 * count)
        + [
            jax.ShapeDtypeStruct((count * tile, hidden), BF16),
            jax.ShapeDtypeStruct((count * tile, hidden), BF16),
            jax.ShapeDtypeStruct((1, hidden), F32),
        ],
        compiler_params=pltpu.CompilerParams(vmem_limit_bytes=60 * 2**20),
        cost_estimate=pl.CostEstimate(
            flops=8 * count * tile * width * hidden,
            bytes_accessed=16 * 2**20,
            transcendentals=count * tile * hidden,
        ),
        name=name,
    )(*(a for a, _ in seconds + grads), bias, before, weights)
    return results[:count], results[count : 2 * count], results[-3], results[-2], results[-1]


def weight_kernel(groups, split, *refs):
    out_ref = refs[-1]
    blocks = sum(groups) * split
    rights = refs[2 * blocks : -1]
    hidden = rights[0].shape[1]
    for side in range(2):
        lefts = refs[side * blocks : (side + 1) * blocks]
        total = None
        at = 0
        for g, count in enumerate(groups):
            rows = [
                jnp.concatenate([r[...] for r in lefts[at + k * split : at + (k + 1) * split]], axis=1)
                for k in range(count)
            ]
            at += count * split
            term = lax.dot_general(
                jnp.concatenate(rows, axis=0),
                rights[side * len(groups) + g][...],
                (((0,), (0,)), ((), ())),
                preferred_element_type=F32,
            )
            total = term if total is None else total + term
        out_ref[:, side * hidden : (side + 1) * hidden] = total.astype(BF16)


def weight_grads(rows, seconds, grads, uppers, actives):
    groups = [len(g) for g in seconds]
    lefts = [b for g in seconds for b in g] + [b for g in grads for b in g]
    width = lefts[0][0].shape[1]
    hidden = uppers[0].shape[1]
    specs = [(a, spec) for a, k in lefts for spec in ring_lanes(rows, width, k)]
    split = len(specs) // len(lefts)
    result = pl.pallas_call(
        functools.partial(weight_kernel, groups, split),
        grid=(width // 256,),
        in_specs=[spec for _, spec in specs]
        + [pl.BlockSpec(r.shape, lambda i: (0, 0)) for r in uppers + actives],
        out_specs=pl.BlockSpec((256, 2 * hidden), lambda i: (i, 0)),
        out_shape=jax.ShapeDtypeStruct((width, 2 * hidden), BF16),
        compiler_params=pltpu.CompilerParams(vmem_limit_bytes=60 * 2**20),
        cost_estimate=pl.CostEstimate(
            flops=2 * len(lefts) * rows * width * hidden,
            bytes_accessed=20 * 2**20,
            transcendentals=0,
        ),
        name="weight_grads",
    )(*(a for a, _ in specs), *uppers, *actives)
    return in_ring(result, width, "weight_order")


def first_kernel(pairs, split, *refs):
    lefts, out_refs = refs[:split], refs[split : 2 * split]
    weight_ref, refs = refs[2 * split], refs[2 * split + 1 :]
    lows, (grad_ref, gain_ref, sums_ref, right_ref) = refs[: 3 * pairs], refs[3 * pairs :]
    wide = lows[0].shape[0]

    @pl.when(pl.program_id(0) == 0)
    def _():
        for c in range(3):
            for pair in range(pairs):
                low = lows[3 * pair + c][...]
                at = (c * pairs + pair) * wide
                right_ref[:, at : at + wide] = low.T if c == 0 else low
        sums_ref[...] = jnp.sum(right_ref[...].astype(F32), axis=0, keepdims=True)

    left = jnp.concatenate([r[...] for r in lefts], axis=1)
    grads = lax.dot_general(
        left, right_ref[...], (((0,), (0,)), ((), ())), preferred_element_type=F32
    )
    width = grads.shape[1]
    grad_ref[:, :width] = grads.astype(BF16)
    grad_ref[:, width:] = jnp.concatenate([r[...] for r in out_refs], axis=0)
    weight = weight_ref[:, :width].astype(F32)
    gain = jnp.sum(weight * grads, axis=1, keepdims=True)
    shift = jnp.sum(weight * sums_ref[...], axis=1, keepdims=True)
    lane = lax.broadcasted_iota(jnp.int32, gain_ref.shape, 1)
    gain_ref[...] = jnp.where(lane == 0, gain, shift)


def first_grads(normed_rows, low, out_sum, weights):
    length, width = normed_rows.shape
    count = lax.axis_size("dp")
    pairs = len(low)
    wide = low[0][0].shape[0]
    lanes = 3 * pairs * wide
    out_wide = out_sum.shape[1]
    lefts = ring_lanes(length, width)
    split = len(lefts)
    if split == 1:
        outs = [pl.BlockSpec((256, out_wide), lambda i: (i, 0))]
        weights = reorder(weights, place_in_ring, "first_order")
    else:
        outs = [
            pl.BlockSpec((width // count, out_wide), lambda i, k=k: (at_ring(2 * i + k, count), 0))
            for k in range(2)
        ]

    def whole(shape):
        return pl.BlockSpec(shape, lambda i: (0, 0))

    flat = [low[pair][c] for pair in range(pairs) for c in range(3)]
    grads, gains, sums = pl.pallas_call(
        functools.partial(first_kernel, pairs, split),
        grid=(width // 256,),
        in_specs=lefts
        + outs
        + [pl.BlockSpec((256, weights.shape[1]), lambda i: (i, 0))]
        + [whole(a.shape) for a in flat],
        out_specs=[
            pl.BlockSpec((256, lanes + out_wide), lambda i: (i, 0)),
            pl.BlockSpec((256, 128), lambda i: (i, 0)),
            whole((1, lanes)),
        ],
        out_shape=[
            jax.ShapeDtypeStruct((width, lanes + out_wide), BF16),
            jax.ShapeDtypeStruct((width, 128), F32),
            jax.ShapeDtypeStruct((1, lanes), F32),
        ],
        scratch_shapes=[pltpu.VMEM((length, lanes), BF16)],
        compiler_params=pltpu.CompilerParams(vmem_limit_bytes=50 * 2**20),
        cost_estimate=pl.CostEstimate(
            flops=2 * length * width * lanes, bytes_accessed=12 * 2**20, transcendentals=0
        ),
        name="first_grads",
    )(*[normed_rows] * split, *[out_sum] * split, weights, *flat)
    gains = gains[:, :2]
    if split == 1:
        return reorder(grads, at_ring, "first_grad_order"), gains, sums
    ring = ring_dp()
    parts = rows_of(gains, count)
    return grads, jnp.concatenate([parts[ring.index(k)] for k in range(count)], axis=0), sums


def fill_bias(bias, masked, slope):
    size = bias.shape[0]
    key = lax.broadcasted_iota(jnp.int32, (size, size), 0)
    query = lax.broadcasted_iota(jnp.int32, (size, size), 1)
    value = key.astype(F32) * slope
    bias[...] = value
    masked[...] = jnp.where(key <= query, value, NEG)


def head_rows(block, head):
    half = block.shape[0] // 2
    rows = lax.broadcasted_iota(jnp.int32, block.shape, 0)
    keep = (rows < half) if head == 0 else (rows >= half)
    return jnp.where(keep, block, jnp.zeros_like(block))


def forward_kernel(
    place, slope_ref, q_ref, k_ref, v_ref, mixed_ref, full_ref, log_ref, bias, masked, values_t, *, scale, pair
):
    query_block = pl.program_id(0)
    me = place[0]
    size = bias.shape[1]
    half = q_ref.shape[0] // 2

    @pl.when(query_block == 0)
    def _():
        values_t[...] = v_ref[...].T
        for head in range(2):
            fill_bias(bias.at[head], masked.at[head], slope_ref[2 * pair + head])

    outputs = []
    logs = []
    for head in range(2):
        step = slope_ref[2 * pair + head] * size
        queries = head_rows(q_ref[...], head)

        def block(key_block, carry, bias_block, head=head, step=step, queries=queries):
            top, total, acc = carry
            at = pl.multiple_of((key_block ^ me) * size, size)
            raw = jnp.dot(k_ref[pl.ds(at, size), :], queries, preferred_element_type=F32)
            scores = raw * scale + bias_block
            base = key_block.astype(F32) * step
            new_top = jnp.maximum(top, jnp.max(scores, axis=0, keepdims=True) + base)
            weights = jnp.exp2(scores - (new_top - base))
            fade = jnp.exp2(top - new_top)
            total = total * fade + jnp.sum(weights, axis=0, keepdims=True)
            rows = values_t[head * half : (head + 1) * half, pl.ds(at, size)]
            acc = acc * fade + jnp.dot(rows, weights.astype(BF16), preferred_element_type=F32)
            return new_top, total, acc

        start = (
            jnp.full((1, size), NEG, F32),
            jnp.zeros((1, size), F32),
            jnp.zeros((half, size), F32),
        )
        carry = lax.fori_loop(
            0, query_block, lambda i, c, head=head, block=block: block(i, c, bias[head]), start
        )
        top, total, acc = block(query_block, carry, masked[head])
        outputs.append(acc / total)
        logs.append(top + jnp.log2(total))
    result = jnp.concatenate(outputs, axis=0)
    full_ref[...] = result
    mixed_ref[...] = result.astype(BF16)
    log_ref[...] = jnp.concatenate(logs, axis=0)


def backward_kernel(
    place,
    slope_ref,
    q_ref,
    k_ref,
    v_ref,
    g_ref,
    full_ref,
    log_ref,
    gq_ref,
    gk_ref,
    gv_ref,
    bias,
    masked,
    gq_acc,
    delta,
    *,
    scale,
    factor,
    pair,
):
    key_block = pl.program_id(0)
    blocks = pl.num_programs(0)
    me = place[0]
    size = bias.shape[1]
    half = q_ref.shape[0] // 2

    @pl.when(key_block == 0)
    def _():
        gq_acc[...] = jnp.zeros_like(gq_acc)
        for head in range(2):
            fill_bias(bias.at[head], masked.at[head], slope_ref[2 * pair + head])
            rows = slice(head * half, (head + 1) * half)
            delta[head : head + 1, :] = jnp.sum(
                g_ref[rows, :].astype(F32) * full_ref[rows, :], axis=0, keepdims=True
            )

    keys = k_ref[...]
    keys_t = keys.T
    values = v_ref[...]
    grad_k = jnp.zeros(keys.shape, F32)
    grad_v = jnp.zeros(keys.shape, F32)
    for head in range(2):
        base = key_block.astype(F32) * (slope_ref[2 * pair + head] * size)
        rows = slice(head * half, (head + 1) * half)

        def block(query_block, carry, bias_block, head=head, base=base, rows=rows):
            grad_k, grad_v = carry
            at = pl.multiple_of((query_block ^ me) * size, size)
            queries = head_rows(q_ref[:, pl.ds(at, size)], head)
            grads = head_rows(g_ref[:, pl.ds(at, size)], head)
            raw = jnp.dot(keys, queries, preferred_element_type=F32)
            log = log_ref[head : head + 1, pl.ds(at, size)] - base
            weights = jnp.exp2(raw * scale + (bias_block - log))
            along = jnp.dot(values, grads, preferred_element_type=F32)
            change = (weights * (along - delta[head : head + 1, pl.ds(at, size)])).astype(BF16)
            contract = (((1,), (1,)), ((), ()))
            grad_v = grad_v + lax.dot_general(
                weights.astype(BF16), grads, contract, preferred_element_type=F32
            )
            grad_k = grad_k + lax.dot_general(change, queries, contract, preferred_element_type=F32)
            gq_acc[rows, pl.ds(at, size)] += jnp.dot(
                keys_t[rows, :], change, preferred_element_type=F32
            )
            return grad_k, grad_v

        carry = block(key_block, (grad_k, grad_v), masked[head])
        grad_k, grad_v = lax.fori_loop(
            key_block + 1, blocks, lambda i, c, head=head, block=block: block(i, c, bias[head]), carry
        )
    low_k = (grad_k * factor).astype(BF16)
    low_v = grad_v.astype(BF16)
    gk_ref[...] = low_k
    gv_ref[...] = low_v

    @pl.when(key_block == blocks - 1)
    def _():
        gq_ref[...] = (gq_acc[...] * factor).astype(BF16)


def attend_forward(place, slopes, queries_t, keys, values, size, head_dim, pair):
    length = queries_t.shape[1]
    wide = 2 * head_dim
    along_q = pl.BlockSpec((wide, size), lambda i, me, s: (pair, i ^ me[0]))
    out_q = pl.BlockSpec((wide, size), lambda i, me, s: (0, i ^ me[0]))
    whole = pl.BlockSpec((length, wide), lambda i, me, s: (0, pair))
    return pl.pallas_call(
        functools.partial(forward_kernel, scale=LOG2E / math.sqrt(head_dim), pair=pair),
        grid_spec=pltpu.PrefetchScalarGridSpec(
            num_scalar_prefetch=2,
            grid=(length // size,),
            in_specs=[along_q, whole, whole],
            out_specs=[out_q, out_q, pl.BlockSpec((2, size), lambda i, me, s: (0, i ^ me[0]))],
            scratch_shapes=[
                pltpu.VMEM((2, size, size), F32),
                pltpu.VMEM((2, size, size), F32),
                pltpu.VMEM((wide, length), BF16),
            ],
        ),
        out_shape=[
            jax.ShapeDtypeStruct((wide, length), BF16),
            jax.ShapeDtypeStruct((wide, length), F32),
            jax.ShapeDtypeStruct((2, length), F32),
        ],
        compiler_params=pltpu.CompilerParams(vmem_limit_bytes=48 * 2**20),
        cost_estimate=pl.CostEstimate(
            flops=10 * 10**9, bytes_accessed=4 * 2**20, transcendentals=5 * 10**6
        ),
        name=f"attend_forward_{pair}",
    )(place, slopes, queries_t, keys, values)


def attend_backward(place, slopes, queries_t, keys, values, grads_t, full, logs, size, head_dim, pair):
    length = queries_t.shape[1]
    wide = 2 * head_dim
    along_k = pl.BlockSpec((size, wide), lambda i, me, s: (i ^ me[0], pair))
    out_k = pl.BlockSpec((size, wide), lambda i, me, s: (i ^ me[0], 0))
    all_q = pl.BlockSpec((wide, length), lambda i, me, s: (pair, 0))
    whole = pl.BlockSpec((wide, length), lambda i, me, s: (0, 0))
    return pl.pallas_call(
        functools.partial(
            backward_kernel,
            scale=LOG2E / math.sqrt(head_dim),
            factor=1.0 / math.sqrt(head_dim),
            pair=pair,
        ),
        grid_spec=pltpu.PrefetchScalarGridSpec(
            num_scalar_prefetch=2,
            grid=(length // size,),
            in_specs=[
                all_q,
                along_k,
                along_k,
                whole,
                whole,
                pl.BlockSpec((2, length), lambda i, me, s: (0, 0)),
            ],
            out_specs=[whole, out_k, out_k],
            scratch_shapes=[
                pltpu.VMEM((2, size, size), F32),
                pltpu.VMEM((2, size, size), F32),
                pltpu.VMEM((wide, length), F32),
                pltpu.VMEM((2, length), F32),
            ],
        ),
        out_shape=[
            jax.ShapeDtypeStruct((wide, length), BF16),
            jax.ShapeDtypeStruct((length, wide), BF16),
            jax.ShapeDtypeStruct((length, wide), BF16),
        ],
        compiler_params=pltpu.CompilerParams(vmem_limit_bytes=48 * 2**20),
        cost_estimate=pl.CostEstimate(
            flops=20 * 10**9, bytes_accessed=6 * 2**20, transcendentals=5 * 10**6
        ),
        name=f"attend_backward_{pair}",
    )(place, slopes, queries_t, keys, values, grads_t, full, logs)


def swap(value, axis, distance):
    size = lax.axis_size(axis)
    return lax.ppermute(value, axis, [(i, i ^ distance) for i in range(size)])


def after(value, *earlier):
    return lax.optimization_barrier((value,) + earlier)[0]


def exchange_blocks(parts):
    return [parts[0]] + [swap(parts[j], "tensor", j) for j in range(1, 4)]


def chip_sum(far, far_near):
    return (far.astype(F32) + swap(far_near, "tensor", 1).astype(F32)).astype(BF16)


def sum_over(value, axes):
    for axis in axes:
        size = lax.axis_size(axis)
        distance = 1
        while distance < size:
            if distance * 4 <= size:
                one, two, three = (swap(value, axis, distance * k) for k in (1, 2, 3))
                value = (value + one) + (two + three)
                distance *= 4
            else:
                value = value + swap(value, axis, distance)
                distance *= 2
    return value


def ring_dp():
    count = lax.axis_size("dp")
    return list(range(0, count, 2)) + list(range(count - 1, 0, -2))


def gather_dp(shard):
    return lax.all_gather(shard, "dp", axis=0, tiled=True, axis_index_groups=[ring_dp()])


def scatter_dp(blocks):
    return lax.psum_scatter(
        blocks, "dp", scatter_dimension=0, tiled=True, axis_index_groups=[ring_dp()]
    ).astype(F32)


def at_ring(place, count):
    return jnp.where(place < count // 2, 2 * place, 2 * (count - 1 - place) + 1)


def place_in_ring(owner, count):
    return jnp.where(owner % 2 == 0, owner // 2, count - 1 - owner // 2)


def reorder(blocks, order, name):
    count = lax.axis_size("dp")
    rows, width = blocks.shape[0] // count, blocks.shape[1]

    def copy(source_ref, result_ref):
        result_ref[...] = source_ref[...]

    return pl.pallas_call(
        copy,
        grid=(count,),
        in_specs=[pl.BlockSpec((rows, width), lambda i: (order(i, count), 0))],
        out_specs=pl.BlockSpec((rows, width), lambda i: (i, 0)),
        out_shape=jax.ShapeDtypeStruct(blocks.shape, blocks.dtype),
        cost_estimate=pl.CostEstimate(
            flops=0, bytes_accessed=4 * count * rows * width, transcendentals=0
        ),
        name=name,
    )(blocks)


def ring_lanes(rows, width, index=0):
    count = lax.axis_size("dp")
    lanes = width // count
    if lanes % 128:
        return [pl.BlockSpec((rows, 256), lambda i: (index, i))]
    return [
        pl.BlockSpec((rows, lanes), lambda i, k=k: (index, at_ring(2 * i + k, count)))
        for k in range(2)
    ]


def in_ring(blocks, width, name):
    if (width // lax.axis_size("dp")) % 128:
        return reorder(blocks, at_ring, name)
    return blocks


def rows_of(value, count):
    size = value.shape[0] // count
    return [value[i * size : (i + 1) * size] for i in range(count)]


def dot(a, b, ca, cb):
    return lax.dot_general(a, b, (((ca,), (cb,)), ((), ())), preferred_element_type=F32)


def body(
    hidden_in,
    norm_gain,
    norm_shift,
    qkv_weight,
    qv_bias,
    out_weight,
    out_bias,
    up_weight,
    up_bias,
    down_weight,
    cotangent,
):
    rows, width = hidden_in.shape
    tensor_size = lax.axis_size("tensor")
    heads_wide = qkv_weight.shape[2]
    hidden_units = up_weight.shape[1]
    local_heads = HEADS // tensor_size
    head_dim = heads_wide // local_heads
    pairs = local_heads // 2
    wide = 2 * head_dim
    me = lax.axis_index("tensor").astype(jnp.int32)
    place = me.reshape(1)
    head_ids = me * local_heads + jnp.arange(local_heads, dtype=jnp.int32)
    slopes = jnp.exp2(-8.0 * (head_ids.astype(F32) + 1.0) / HEADS) * LOG2E
    part = rows // 2
    stat = functools.partial(row_call, rows=rows, width=width)
    row_f32 = jax.ShapeDtypeStruct((rows, width), F32)
    row_bf16 = jax.ShapeDtypeStruct((rows, width), BF16)
    part_bf16 = jax.ShapeDtypeStruct((part, width), BF16)
    four_f32 = jax.ShapeDtypeStruct((4, width), F32)

    first_shard = jnp.concatenate(
        [qkv_weight[0], qkv_weight[1], qkv_weight[2], out_weight.T], axis=1
    )
    second_shard = jnp.concatenate([up_weight, down_weight.T], axis=1)
    first_ring = gather_dp(first_shard)
    first_full = reorder(first_ring, place_in_ring, "first_weights")
    second_weights = gather_dp(second_shard)

    (normed,) = stat(
        first_norm_kernel, arrays=[hidden_in, norm_gain, norm_shift], outs=[row_bf16], name="norm_one"
    )
    normed_far = swap(normed, "tensor", 2)
    normed_near = swap(normed, "tensor", 1)
    normed_rows = jnp.concatenate(
        [normed, normed_near, normed_far, swap(normed_far, "tensor", 1)], axis=0
    )
    grads_far = swap(cotangent, "tensor", 2)
    grads_near = swap(cotangent, "tensor", 1)
    grads_far_near = swap(grads_far, "tensor", 1)

    w_query, w_key, w_value = (
        first_full[:, c * heads_wide : (c + 1) * heads_wide] for c in range(3)
    )
    queries_t = (dot(w_query, normed_rows, 0, 1) + qv_bias[0][:, None]).astype(BF16)
    keys = dot(normed_rows, w_key, 1, 0).astype(BF16)
    values = (dot(normed_rows, w_value, 1, 0) + qv_bias[1]).astype(BF16)
    out_mine = first_full[:, 3 * heads_wide :]
    out_far = swap(out_mine, "tensor", 2)
    kept = []
    mixed_parts = [[] for _ in range(tensor_size)]
    received = out_far
    for pair in range(pairs):
        mixed_t, mixed_full, logs = attend_forward(
            place,
            slopes,
            queries_t
            if pair == 0
            else after(queries_t, grads_far, mixed_full),
            keys,
            values,
            rows,
            head_dim,
            pair,
        )
        if pair > 0:
            mixed_t = after(mixed_t, *received, out_far)
        kept.append((mixed_full, logs))
        parts = [mixed_t[:, j * rows : (j + 1) * rows] for j in range(tensor_size)]
        received = exchange_blocks(parts)
        for j, block in enumerate(received):
            mixed_parts[j].append(block)
    out_full = jnp.concatenate(
        [out_mine, swap(out_mine, "tensor", 1), out_far, swap(out_far, "tensor", 1)], axis=1
    )
    mixed_all = jnp.concatenate([block for group in mixed_parts for block in group], axis=0)
    attn_sum = dot(mixed_all, out_full, 0, 1)
    middle, second = stat(
        second_norm_kernel,
        arrays=[hidden_in, attn_sum, out_bias, norm_gain, norm_shift],
        outs=[row_f32, (part_bf16, part_bf16)],
        name="norm_two",
    )

    up_bias_row = up_bias.reshape(1, hidden_units)
    far_chunks = [swap(second[c], "tensor", 2) for c in range(2)]
    seconds = [[(block, 0) for block in second]]
    seconds[0] += [(swap(block, "tensor", 1), 0) for block in second]
    grads = [[(g, c) for g in (cotangent, grads_near) for c in range(2)]]
    mlp_a, back_a, active, upper, sums_up = feed(
        part, seconds[0], grads[0], second_weights, up_bias_row, jnp.zeros_like(up_bias_row), "feed_near"
    )
    actives, uppers = [active], [upper]
    mlps, back_fars = [], []
    earlier = (mlp_a[0],)
    for c in range(2):
        far = after(far_chunks[c], *earlier)
        pair_c = [(far, 0), (swap(far, "tensor", 1), 0)]
        if c > 0:
            pair_c[0] = (after(far, mine), 0)
        grads_c = [(grads_far, c), (grads_far_near, c)]
        mlp_c, back_c, active, upper, sums_up = feed(
            part, pair_c, grads_c, second_weights, up_bias_row, sums_up, f"feed_far_{c}"
        )
        earlier = (mlp_c[0],)
        seconds.append(pair_c)
        grads.append(grads_c)
        actives.append(active)
        uppers.append(upper)
        mlps.append(mlp_c)
        mine = chip_sum(back_c[0], after(back_c[1], *back_fars))
        back_fars.append(swap(mine, "tensor", 2))
    back_near = tuple(swap(back_a[2 + c], "tensor", 1) for c in range(2))

    uppers[0] = after(uppers[0], back_fars[0], mine)
    grad_second_w = weight_grads(part, seconds, grads, uppers, actives)
    local_second_w = grad_second_w
    grad_second_w = scatter_dp(grad_second_w)
    grad_up_weight = grad_second_w[:, :hidden_units]
    grad_down_weight = grad_second_w[:, hidden_units:].T

    grad_middle, grad_attn, early = stat(
        second_back_kernel,
        arrays=[after(middle, local_second_w), cotangent, tuple(back_a[:2]), back_near, tuple(back_fars), norm_gain],
        outs=[row_f32, row_bf16, four_f32],
        name="norm_two_back",
    )
    mixed_grads = dot(out_full, grad_attn, 0, 1).astype(BF16)
    mlps = [lax.optimization_barrier((*m, grad_attn))[:2] for m in mlps]
    mlp_a = lax.optimization_barrier((*mlp_a, grad_attn))[:4]
    grads_t = []
    for pair in range(pairs):
        parts = [
            mixed_grads[j * heads_wide + pair * wide : j * heads_wide + (pair + 1) * wide]
            for j in range(tensor_size)
        ]
        if pair > 0:
            parts = [after(p, grads_t[-1]) for p in parts]
        grads_t.append(jnp.concatenate(exchange_blocks(parts), axis=1))

    out_partial = dot(after(grad_attn, mixed_grads), mixed_all, 0, 1).astype(BF16)
    out_cols = [out_partial[:, j * heads_wide : (j + 1) * heads_wide] for j in range(tensor_size)]
    out_mine_sum = chip_sum(out_cols[2], out_cols[3])
    out_far_sum = swap(out_mine_sum, "tensor", 2)
    mlp_mine_sum = jnp.concatenate([chip_sum(m[0], m[1]) for m in mlps], axis=0)
    mlp_far = swap(after(mlp_mine_sum, out_far_sum), "tensor", 2)
    mlp_near = jnp.concatenate([swap(m, "tensor", 1) for m in mlp_a[2:]], axis=0)
    mlp_own = jnp.concatenate(mlp_a[:2], axis=0)
    low = []
    for pair in range(pairs):
        grads_pair = grads_t[pair]
        if pair == 0:
            grads_pair = after(grads_pair, out_mine_sum, mlp_mine_sum)
        else:
            grads_pair = after(grads_pair, low[-1][0], out_far_sum)
        mixed_full, logs = kept[pair]
        low.append(
            attend_backward(
                place, slopes, queries_t, keys, values, grads_pair, mixed_full, logs, rows, head_dim, pair
            )
        )
    low[-1] = lax.optimization_barrier((*low[-1], mlp_far))[:3]
    out_sum = (
        out_cols[0].astype(F32)
        + swap(out_cols[1], "tensor", 1).astype(F32)
        + out_far_sum.astype(F32)
    ).astype(BF16)
    send, gains, column_sums = first_grads(normed_rows, low, out_sum, first_ring)
    first_sums = scatter_dp(after(send, grad_second_w))

    query_low = after(jnp.concatenate([g[0] for g in low], axis=0), send)
    key_low = jnp.concatenate([g[1] for g in low], axis=1)
    value_low = jnp.concatenate([g[2] for g in low], axis=1)

    def normed_grads(at, query_low):
        return (
            dot(query_low[:, at], w_query, 0, 1)
            + dot(key_low[at], w_key, 1, 1)
            + dot(value_low[at], w_value, 1, 1)
        ).astype(BF16)

    half = 2 * rows
    far_grads = normed_grads(slice(half, 2 * half), query_low)
    first_mine = chip_sum(far_grads[:rows], far_grads[rows:])
    first_far = swap(first_mine, "tensor", 2)
    near_grads = normed_grads(slice(0, half), after(query_low, first_mine))
    first_near = swap(near_grads[rows:], "tensor", 1)

    grad_qkv = jnp.stack([first_sums[:, c * heads_wide : (c + 1) * heads_wide] for c in range(3)])
    grad_out_weight = first_sums[:, 3 * heads_wide :].T

    (grad_in,) = stat(
        first_back_kernel,
        arrays=[hidden_in, grad_middle, near_grads[:rows], first_near, first_far, norm_gain],
        outs=[row_f32],
        name="norm_one_back",
    )
    block_out = (
        after(middle, near_grads)
        + (mlp_own.astype(F32) + mlp_near.astype(F32) + mlp_far.astype(F32))
        + out_bias[1]
    )

    shift_sum = gains[:, 1]
    gain_sum = (gains[:, 0] - norm_shift[0] * shift_sum) / norm_gain[0]
    lanes = 128
    whole_sums = jnp.concatenate([early, gain_sum[None], shift_sum[None]], axis=0).reshape(-1, lanes)
    columns = column_sums[0]
    split_sums = after(
        jnp.concatenate([columns[:heads_wide], columns[2 * heads_wide :], sums_up[0]]), near_grads
    ).reshape(-1, lanes)
    sums = sum_over(jnp.concatenate([whole_sums, split_sums], axis=0), ("dp",))
    whole_sums = sum_over(sums[: whole_sums.shape[0]], ("tensor",)).reshape(-1, width)
    split_sums = sums[whole_sums.size // lanes :].reshape(-1)
    return (
        block_out,
        grad_in,
        jnp.stack([whole_sums[4], whole_sums[0]]),
        jnp.stack([whole_sums[5], whole_sums[1]]),
        grad_qkv,
        split_sums[: 2 * heads_wide].reshape(2, heads_wide),
        grad_out_weight,
        whole_sums[2:4],
        grad_up_weight,
        split_sums[2 * heads_wide :],
        grad_down_weight,
    )


def solution(mesh):
    return jax.shard_map(
        body,
        mesh=mesh,
        in_specs=(
            P(("dp", "tensor"), None),
            P(),
            P(),
            P(None, "dp", "tensor"),
            P(None, "tensor"),
            P("tensor", "dp"),
            P(),
            P("dp", "tensor"),
            P("tensor"),
            P("tensor", "dp"),
            P(("dp", "tensor"), None),
        ),
        out_specs=(
            P(("dp", "tensor"), None),
            P(("dp", "tensor"), None),
            P(),
            P(),
            P(None, "dp", "tensor"),
            P(None, "tensor"),
            P("tensor", "dp"),
            P(),
            P("dp", "tensor"),
            P("tensor"),
            P("tensor", "dp"),
        ),
        check_vma=False,
    )
```

```python
import functools
import math

import jax
import jax.numpy as jnp
from jax import lax
from jax.experimental import pallas as pl
from jax.experimental.pallas import tpu as pltpu
from jax.sharding import PartitionSpec as P

HEADS = 16
LOG2E = 1.4426950408889634
NEG = -1e30
BF16 = jnp.bfloat16
F32 = jnp.float32


def normalise(values):
    average = jnp.mean(values, axis=-1, keepdims=True)
    centered = values - average
    inverse = lax.rsqrt(jnp.mean(centered * centered, axis=-1, keepdims=True) + 1e-05)
    return centered * inverse, inverse


def gelu_both(values):
    first = 0.7978845608
    square = values * values
    tangent = jnp.tanh(values * (first + (first * 0.044715) * square))
    half = 0.5 + 0.5 * tangent
    active = values * half
    slope = half + (values - values * (tangent * tangent)) * (
        0.5 * first + (1.5 * 0.044715 * first) * square
    )
    return active, slope


def first_norm_kernel(hidden, gain, shift, put_normed):
    scaled, _ = normalise(hidden().astype(F32))
    put_normed((scaled * gain()[0:1, :] + shift()[0:1, :]).astype(BF16))


def second_norm_kernel(hidden, attn, bias, gain, shift, put_middle, put_normed):
    middle = hidden().astype(F32) + attn() + bias()[0:1, :]
    put_middle(middle)
    scaled, _ = normalise(middle)
    put_normed((scaled * gain()[1:2, :] + shift()[1:2, :]).astype(BF16))


def back_of_norm(value, own, near, far, gain):
    scaled, inverse = normalise(value.astype(F32))
    gradient = own.astype(F32) + near.astype(F32) + far.astype(F32)
    grad_scaled = gradient * gain
    grad_mean = jnp.mean(grad_scaled, axis=-1, keepdims=True)
    grad_proj = jnp.mean(grad_scaled * scaled, axis=-1, keepdims=True)
    return inverse * (grad_scaled - grad_mean - scaled * grad_proj), gradient, scaled


def second_back_kernel(middle, above, own, near, far, gain, put_total, put_low, add_sums):
    change, gradient, scaled = back_of_norm(middle(), own(), near(), far(), gain()[1:2, :])
    grads = above().astype(F32)
    total = grads + change
    put_total(total)
    put_low(total.astype(BF16))
    columns = [gradient * scaled, gradient, total, grads]
    add_sums(jnp.concatenate([jnp.sum(c, axis=0, keepdims=True) for c in columns], axis=0))


def first_back_kernel(hidden, above, own, near, far, gain, put_total):
    change, _, _ = back_of_norm(hidden(), own(), near(), far(), gain()[0:1, :])
    put_total(above() + change)


def block_kernel(middle, own, near, far, bias, put_block):
    mlp = own().astype(F32) + near().astype(F32) + far().astype(F32)
    put_block(middle() + mlp + bias()[1:2, :])


def row_call(kernel, rows, width, arrays, outs, name, tile=256):
    tile = min(tile, rows // 2)
    half = rows // 2 // tile

    def specs(array):
        if isinstance(array, tuple):
            return [
                pl.BlockSpec((tile, width), lambda i: (jnp.minimum(i, half - 1), 0)),
                pl.BlockSpec((tile, width), lambda i: (jnp.maximum(i - half, 0), 0)),
            ]
        if array.shape[0] == rows:
            return [pl.BlockSpec((tile, width), lambda i: (i, 0))]
        return [pl.BlockSpec(array.shape, lambda i: (0, 0))]

    def flat(values):
        return [v for value in values for v in (value if isinstance(value, tuple) else (value,))]

    def run(*refs):
        step = pl.program_id(0)
        at = 0
        accesses = []
        for k, value in enumerate(arrays + outs):
            reads = k < len(arrays)
            if isinstance(value, tuple):
                one, two = refs[at : at + 2]
                at += 2
                if reads:
                    accesses.append(lambda a=one, b=two: jnp.where(step < half, a[...], b[...]))
                else:

                    def put(block, a=one, b=two):
                        @pl.when(step < half)
                        def _():
                            a[...] = block

                        @pl.when(step >= half)
                        def _():
                            b[...] = block

                    accesses.append(put)
                continue
            ref = refs[at]
            at += 1
            if reads:
                accesses.append(lambda a=ref: a[...])
            elif value.shape[0] == rows:

                def put(block, a=ref):
                    a[...] = block

                accesses.append(put)
            else:

                def add(block, a=ref):
                    @pl.when(step == 0)
                    def _():
                        a[...] = block

                    @pl.when(step > 0)
                    def _():
                        a[...] += block

                accesses.append(add)
        kernel(*accesses)

    results = pl.pallas_call(
        run,
        grid=(2 * half,),
        in_specs=[spec for a in arrays for spec in specs(a)],
        out_specs=[spec for o in outs for spec in specs(o)],
        out_shape=flat(outs),
        compiler_params=pltpu.CompilerParams(vmem_limit_bytes=32 * 2**20),
        cost_estimate=pl.CostEstimate(
            flops=20 * rows * width, bytes_accessed=12 * rows * width, transcendentals=rows
        ),
        name=name,
    )(*flat(arrays))
    results = list(results)
    return [
        (results.pop(0), results.pop(0)) if isinstance(o, tuple) else results.pop(0) for o in outs
    ]


def feed_kernel(count, ring, *refs):
    seconds, grads = refs[:count], refs[count : 2 * count]
    bias_ref, before_ref = refs[2 * count : 2 * count + 2]
    parts, refs = refs[2 * count + 2], refs[2 * count + 3 :]
    mlps, backs = refs[:count], refs[count : 2 * count]
    active_ref, upper_ref, sums_ref, weight_ref, arrived = refs[2 * count :]
    hidden = bias_ref.shape[1]
    up_ref, down_ref = weight_ref.at[:, :hidden], weight_ref.at[:, hidden:]
    step = pl.program_id(0)
    contract = (((1,), (1,)), ((), ()))

    @pl.when(step == 0)
    def _():
        sums_ref[...] = before_ref[...]
        rows = parts.shape[0] // len(ring)
        copies = [
            pltpu.make_async_copy(
                parts.at[at * rows : (at + 1) * rows, :],
                weight_ref.at[owner * rows : (owner + 1) * rows, :],
                arrived.at[at],
            )
            for at, owner in enumerate(ring)
        ]
        for copy in copies:
            copy.start()
        for copy in copies:
            copy.wait()

    for k in range(count):

        @pl.when(step == k)
        def _(k=k):
            upper = jnp.dot(seconds[k][...], up_ref[...], preferred_element_type=F32) + bias_ref[...]
            active, slope = gelu_both(upper)
            active = active.astype(BF16)
            active_ref[...] = active
            grad_active = jnp.dot(grads[k][...], down_ref[...], preferred_element_type=F32)
            grad_upper = (grad_active * slope).astype(BF16)
            upper_ref[...] = grad_upper
            backs[k][...] = lax.dot_general(
                grad_upper, up_ref[...], contract, preferred_element_type=F32
            ).astype(BF16)
            mlps[k][...] = lax.dot_general(
                active, down_ref[...], contract, preferred_element_type=F32
            ).astype(BF16)
            sums_ref[...] += jnp.sum(grad_upper.astype(F32), axis=0, keepdims=True)


def feed(tile, seconds, grads, weights, bias, before, name):
    count, ring = len(seconds), ring_dp()
    width = seconds[0][0].shape[1]
    hidden = bias.shape[1]
    block = pl.BlockSpec((tile, width), lambda i: (0, 0))

    def at(k):
        return pl.BlockSpec((tile, width), lambda i: (k, 0))

    by_hidden = pl.BlockSpec((tile, hidden), lambda i: (i, 0))
    row = pl.BlockSpec((1, hidden), lambda i: (0, 0))
    results = pl.pallas_call(
        functools.partial(feed_kernel, count, ring),
        grid=(count,),
        in_specs=[at(k) for _, k in seconds + grads]
        + [row, row, pl.BlockSpec(memory_space=pl.ANY)],
        out_specs=[block] * (2 * count) + [by_hidden, by_hidden, row],
        scratch_shapes=[
            pltpu.VMEM((width, 2 * hidden), BF16),
            pltpu.SemaphoreType.DMA((len(ring),)),
        ],
        out_shape=[jax.ShapeDtypeStruct((tile, width), BF16)] * (2 * count)
        + [
            jax.ShapeDtypeStruct((count * tile, hidden), BF16),
            jax.ShapeDtypeStruct((count * tile, hidden), BF16),
            jax.ShapeDtypeStruct((1, hidden), F32),
        ],
        compiler_params=pltpu.CompilerParams(vmem_limit_bytes=36 * 2**20),
        cost_estimate=pl.CostEstimate(
            flops=8 * count * tile * width * hidden,
            bytes_accessed=16 * 2**20,
            transcendentals=count * tile * hidden,
        ),
        name=name,
    )(*(a for a, _ in seconds + grads), bias, before, weights)
    return results[:count], results[count : 2 * count], results[-3], results[-2], results[-1]


def weight_kernel(groups, split, *refs):
    out_ref = refs[-1]
    blocks = sum(groups) * split
    rights = refs[2 * blocks : -1]
    hidden = rights[0].shape[1]
    for side in range(2):
        lefts = refs[side * blocks : (side + 1) * blocks]
        total = None
        at = 0
        for g, count in enumerate(groups):
            rows = [
                jnp.concatenate([r[...] for r in lefts[at + k * split : at + (k + 1) * split]], axis=1)
                for k in range(count)
            ]
            at += count * split
            term = lax.dot_general(
                jnp.concatenate(rows, axis=0),
                rights[side * len(groups) + g][...],
                (((0,), (0,)), ((), ())),
                preferred_element_type=F32,
            )
            total = term if total is None else total + term
        out_ref[:, side * hidden : (side + 1) * hidden] = total.astype(BF16)


def weight_grads(rows, seconds, grads, uppers, actives):
    groups = [len(g) for g in seconds]
    lefts = [b for g in seconds for b in g] + [b for g in grads for b in g]
    width = lefts[0][0].shape[1]
    hidden = uppers[0].shape[1]
    specs = [(a, spec) for a, k in lefts for spec in ring_lanes(rows, width, k)]
    split = len(specs) // len(lefts)
    result = pl.pallas_call(
        functools.partial(weight_kernel, groups, split),
        grid=(width // 256,),
        in_specs=[spec for _, spec in specs]
        + [pl.BlockSpec(r.shape, lambda i: (0, 0)) for r in uppers + actives],
        out_specs=pl.BlockSpec((256, 2 * hidden), lambda i: (i, 0)),
        out_shape=jax.ShapeDtypeStruct((width, 2 * hidden), BF16),
        compiler_params=pltpu.CompilerParams(vmem_limit_bytes=36 * 2**20),
        cost_estimate=pl.CostEstimate(
            flops=2 * len(lefts) * rows * width * hidden,
            bytes_accessed=20 * 2**20,
            transcendentals=0,
        ),
        name="weight_grads",
    )(*(a for a, _ in specs), *uppers, *actives)
    return in_ring(result, width, "weight_order")


def join_kernel(pairs, *refs):
    lows, (joined_ref, sums_ref) = refs[: 3 * pairs], refs[3 * pairs :]
    wide = lows[0].shape[0]
    for c in range(3):
        for pair in range(pairs):
            low = lows[3 * pair + c][...]
            at = (c * pairs + pair) * wide
            joined_ref[:, at : at + wide] = low.T if c == 0 else low
    sums = jnp.sum(joined_ref[...].astype(F32), axis=0, keepdims=True)

    @pl.when(pl.program_id(0) == 0)
    def _():
        sums_ref[...] = sums

    @pl.when(pl.program_id(0) > 0)
    def _():
        sums_ref[...] += sums


def join_low(low):
    pairs = len(low)
    wide, length = low[0][0].shape
    lanes = 3 * pairs * wide
    tile = min(512, length)
    specs = [
        pl.BlockSpec((wide, tile), lambda i: (0, i)),
        pl.BlockSpec((tile, wide), lambda i: (i, 0)),
        pl.BlockSpec((tile, wide), lambda i: (i, 0)),
    ]
    return pl.pallas_call(
        functools.partial(join_kernel, pairs),
        grid=(length // tile,),
        in_specs=specs * pairs,
        out_specs=[
            pl.BlockSpec((tile, lanes), lambda i: (i, 0)),
            pl.BlockSpec((1, lanes), lambda i: (0, 0)),
        ],
        out_shape=[
            jax.ShapeDtypeStruct((length, lanes), BF16),
            jax.ShapeDtypeStruct((1, lanes), F32),
        ],
        compiler_params=pltpu.CompilerParams(vmem_limit_bytes=32 * 2**20),
        cost_estimate=pl.CostEstimate(
            flops=length * lanes, bytes_accessed=4 * length * lanes, transcendentals=0
        ),
        name="join_low",
    )(*(g for group in low for g in group))


def first_kernel(blocks, split, *refs):
    lefts, refs = refs[: blocks * split], refs[blocks * split :]
    outs, (right_ref, sums_ref, weight_ref, grad_ref, gain_ref) = refs[:split], refs[split:]
    left = jnp.concatenate(
        [
            jnp.concatenate([r[...] for r in lefts[k * split : (k + 1) * split]], axis=1)
            for k in range(blocks)
        ],
        axis=0,
    )
    grads = lax.dot_general(
        left, right_ref[...], (((0,), (0,)), ((), ())), preferred_element_type=F32
    )
    width = grads.shape[1]
    grad_ref[:, :width] = grads.astype(BF16)
    grad_ref[:, width:] = jnp.concatenate([r[...] for r in outs], axis=0)
    weight = weight_ref[:, :width].astype(F32)
    gain = jnp.sum(weight * grads, axis=1, keepdims=True)
    shift = jnp.sum(weight * sums_ref[...], axis=1, keepdims=True)
    lane = lax.broadcasted_iota(jnp.int32, gain_ref.shape, 1)
    gain_ref[...] = jnp.where(lane == 0, gain, shift)


def first_grads(normed_blocks, joined, sums, out_sum, weights):
    rows, width = normed_blocks[0].shape
    length, lanes = joined.shape
    count = lax.axis_size("dp")
    out_wide = out_sum.shape[1]
    lefts = ring_lanes(rows, width)
    split = len(lefts)
    if split == 1:
        outs = [pl.BlockSpec((256, out_wide), lambda i: (i, 0))]
        weights = reorder(weights, place_in_ring, "first_order")
    else:
        outs = [
            pl.BlockSpec((width // count, out_wide), lambda i, k=k: (at_ring(2 * i + k, count), 0))
            for k in range(2)
        ]

    def whole(shape):
        return pl.BlockSpec(shape, lambda i: (0, 0))

    grads, gains = pl.pallas_call(
        functools.partial(first_kernel, len(normed_blocks), split),
        grid=(width // 256,),
        in_specs=lefts * len(normed_blocks)
        + outs
        + [
            whole(joined.shape),
            whole(sums.shape),
            pl.BlockSpec((256, weights.shape[1]), lambda i: (i, 0)),
        ],
        out_specs=[
            pl.BlockSpec((256, lanes + out_wide), lambda i: (i, 0)),
            pl.BlockSpec((256, 128), lambda i: (i, 0)),
        ],
        out_shape=[
            jax.ShapeDtypeStruct((width, lanes + out_wide), BF16),
            jax.ShapeDtypeStruct((width, 128), F32),
        ],
        compiler_params=pltpu.CompilerParams(vmem_limit_bytes=50 * 2**20),
        cost_estimate=pl.CostEstimate(
            flops=2 * length * width * lanes, bytes_accessed=12 * 2**20, transcendentals=0
        ),
        name="first_grads",
    )(
        *(b for block in normed_blocks for b in [block] * split),
        *[out_sum] * split,
        joined,
        sums,
        weights,
    )
    gains = gains[:, :2]
    if split == 1:
        return reorder(grads, at_ring, "first_grad_order"), gains
    ring = ring_dp()
    parts = rows_of(gains, count)
    return grads, jnp.concatenate([parts[ring.index(k)] for k in range(count)], axis=0)


def fill_bias(bias, masked, slope):
    size = bias.shape[0]
    key = lax.broadcasted_iota(jnp.int32, (size, size), 0)
    query = lax.broadcasted_iota(jnp.int32, (size, size), 1)
    value = key.astype(F32) * slope
    bias[...] = value
    masked[...] = jnp.where(key <= query, value, NEG)


def head_rows(block, head):
    half = block.shape[0] // 2
    rows = lax.broadcasted_iota(jnp.int32, block.shape, 0)
    keep = (rows < half) if head == 0 else (rows >= half)
    return jnp.where(keep, block, jnp.zeros_like(block))


def forward_kernel(
    place, slope_ref, q_ref, k_ref, v_ref, mixed_ref, full_ref, log_ref, bias, masked, values_t, *, scale, pair
):
    query_block = pl.program_id(0)
    me = place[0]
    size = bias.shape[1]
    half = q_ref.shape[0] // 2

    @pl.when(query_block == 0)
    def _():
        values_t[...] = v_ref[...].T
        for head in range(2):
            fill_bias(bias.at[head], masked.at[head], slope_ref[2 * pair + head])

    outputs = []
    logs = []
    for head in range(2):
        step = slope_ref[2 * pair + head] * size
        queries = head_rows(q_ref[...], head)

        def block(key_block, carry, bias_block, queries, count=size, head=head, step=step):
            top, total, acc = carry
            at = pl.multiple_of((key_block ^ me) * size, size)
            raw = jnp.dot(k_ref[pl.ds(at, count), :], queries, preferred_element_type=F32)
            scores = raw * scale + bias_block
            base = key_block.astype(F32) * step
            new_top = jnp.maximum(top, jnp.max(scores, axis=0, keepdims=True) + base)
            weights = jnp.exp2(scores - (new_top - base))
            fade = jnp.exp2(top - new_top)
            total = total * fade + jnp.sum(weights, axis=0, keepdims=True)
            rows = values_t[head * half : (head + 1) * half, pl.ds(at, count)]
            acc = acc * fade + jnp.dot(rows, weights.astype(BF16), preferred_element_type=F32)
            return new_top, total, acc

        start = (
            jnp.full((1, size), NEG, F32),
            jnp.zeros((1, size), F32),
            jnp.zeros((half, size), F32),
        )
        carry = lax.fori_loop(
            0,
            query_block,
            lambda i, c, head=head, block=block, queries=queries: block(i, c, bias[head], queries),
            start,
        )
        middle = size // 2
        one = block(
            query_block,
            tuple(c[:, :middle] for c in carry),
            masked[head, :middle, :middle],
            queries[:, :middle],
            middle,
        )
        two = block(
            query_block,
            tuple(c[:, middle:] for c in carry),
            masked[head, :, middle:],
            queries[:, middle:],
        )
        top, total, acc = (jnp.concatenate(c, axis=1) for c in zip(one, two))
        outputs.append(acc / total)
        logs.append(top + jnp.log2(total))
    result = jnp.concatenate(outputs, axis=0)
    full_ref[...] = result
    mixed_ref[...] = result.astype(BF16)
    log_ref[...] = jnp.concatenate(logs, axis=0)


def backward_kernel(
    place,
    slope_ref,
    q_ref,
    k_ref,
    v_ref,
    g_ref,
    full_ref,
    log_ref,
    gq_ref,
    gk_ref,
    gv_ref,
    bias,
    masked,
    gq_acc,
    delta,
    *,
    scale,
    factor,
    pair,
):
    key_block = pl.program_id(0)
    blocks = pl.num_programs(0)
    me = place[0]
    size = bias.shape[1]
    half = q_ref.shape[0] // 2

    @pl.when(key_block == 0)
    def _():
        gq_acc[...] = jnp.zeros_like(gq_acc)
        for head in range(2):
            fill_bias(bias.at[head], masked.at[head], slope_ref[2 * pair + head])
            rows = slice(head * half, (head + 1) * half)
            delta[head : head + 1, :] = jnp.sum(
                g_ref[rows, :].astype(F32) * full_ref[rows, :], axis=0, keepdims=True
            )

    keys = k_ref[...]
    keys_t = keys.T
    values = v_ref[...]
    grad_k = jnp.zeros(keys.shape, F32)
    grad_v = jnp.zeros(keys.shape, F32)
    for head in range(2):
        base = key_block.astype(F32) * (slope_ref[2 * pair + head] * size)
        rows = slice(head * half, (head + 1) * half)

        def block(query_block, carry, bias_block, skip, count, head=head, base=base, rows=rows):
            grad_k, grad_v = carry
            seen, wide = bias_block.shape
            at = pl.multiple_of((query_block ^ me) * size + skip, size if skip == 0 else skip)
            queries = head_rows(q_ref[:, pl.ds(at, wide)], head)
            grads = head_rows(g_ref[:, pl.ds(at, wide)], head)
            raw = jnp.dot(keys[:seen], queries, preferred_element_type=F32)
            log = log_ref[head : head + 1, pl.ds(at, wide)] - base
            weights = jnp.exp2(raw * scale + (bias_block - log))
            along = jnp.dot(values[:seen], grads, preferred_element_type=F32)
            change = (weights * (along - delta[head : head + 1, pl.ds(at, wide)])).astype(BF16)
            contract = (((1,), (1,)), ((), ()))
            more_v = lax.dot_general(
                weights.astype(BF16), grads, contract, preferred_element_type=F32
            )
            more_k = lax.dot_general(change, queries, contract, preferred_element_type=F32)
            gq_acc[rows, pl.ds(at, wide)] += jnp.dot(
                keys_t[rows, :seen], change, preferred_element_type=F32
            )
            if seen == count:
                return grad_k + more_k, grad_v + more_v
            return tuple(
                jnp.concatenate([g[:seen] + m, g[seen:]], axis=0)
                for g, m in ((grad_k, more_k), (grad_v, more_v))
            )

        middle = size // 2
        carry = block(key_block, (grad_k, grad_v), masked[head, :middle, :middle], 0, size)
        carry = block(key_block, carry, masked[head, :, middle:], middle, size)
        grad_k, grad_v = lax.fori_loop(
            key_block + 1,
            blocks,
            lambda i, c, head=head, block=block: block(i, c, bias[head], 0, size),
            carry,
        )
    low_k = (grad_k * factor).astype(BF16)
    low_v = grad_v.astype(BF16)
    gk_ref[...] = low_k
    gv_ref[...] = low_v

    @pl.when(key_block == blocks - 1)
    def _():
        gq_ref[...] = (gq_acc[...] * factor).astype(BF16)


def attend_forward(place, slopes, queries_t, keys, values, size, head_dim, pair):
    length = queries_t.shape[1]
    wide = 2 * head_dim
    along_q = pl.BlockSpec((wide, size), lambda i, me, s: (pair, i ^ me[0]))
    out_q = pl.BlockSpec((wide, size), lambda i, me, s: (0, i ^ me[0]))
    whole = pl.BlockSpec((length, wide), lambda i, me, s: (0, pair))
    return pl.pallas_call(
        functools.partial(forward_kernel, scale=LOG2E / math.sqrt(head_dim), pair=pair),
        grid_spec=pltpu.PrefetchScalarGridSpec(
            num_scalar_prefetch=2,
            grid=(length // size,),
            in_specs=[along_q, whole, whole],
            out_specs=[out_q, out_q, pl.BlockSpec((2, size), lambda i, me, s: (0, i ^ me[0]))],
            scratch_shapes=[
                pltpu.VMEM((2, size, size), F32),
                pltpu.VMEM((2, size, size), F32),
                pltpu.VMEM((wide, length), BF16),
            ],
        ),
        out_shape=[
            jax.ShapeDtypeStruct((wide, length), BF16),
            jax.ShapeDtypeStruct((wide, length), F32),
            jax.ShapeDtypeStruct((2, length), F32),
        ],
        compiler_params=pltpu.CompilerParams(vmem_limit_bytes=48 * 2**20),
        cost_estimate=pl.CostEstimate(
            flops=10 * 10**9, bytes_accessed=4 * 2**20, transcendentals=5 * 10**6
        ),
        name=f"attend_forward_{pair}",
    )(place, slopes, queries_t, keys, values)


def attend_backward(place, slopes, queries_t, keys, values, grads_t, full, logs, size, head_dim, pair):
    length = queries_t.shape[1]
    wide = 2 * head_dim
    along_k = pl.BlockSpec((size, wide), lambda i, me, s: (i ^ me[0], pair))
    out_k = pl.BlockSpec((size, wide), lambda i, me, s: (i ^ me[0], 0))
    all_q = pl.BlockSpec((wide, length), lambda i, me, s: (pair, 0))
    whole = pl.BlockSpec((wide, length), lambda i, me, s: (0, 0))
    return pl.pallas_call(
        functools.partial(
            backward_kernel,
            scale=LOG2E / math.sqrt(head_dim),
            factor=1.0 / math.sqrt(head_dim),
            pair=pair,
        ),
        grid_spec=pltpu.PrefetchScalarGridSpec(
            num_scalar_prefetch=2,
            grid=(length // size,),
            in_specs=[
                all_q,
                along_k,
                along_k,
                whole,
                whole,
                pl.BlockSpec((2, length), lambda i, me, s: (0, 0)),
            ],
            out_specs=[whole, out_k, out_k],
            scratch_shapes=[
                pltpu.VMEM((2, size, size), F32),
                pltpu.VMEM((2, size, size), F32),
                pltpu.VMEM((wide, length), F32),
                pltpu.VMEM((2, length), F32),
            ],
        ),
        out_shape=[
            jax.ShapeDtypeStruct((wide, length), BF16),
            jax.ShapeDtypeStruct((length, wide), BF16),
            jax.ShapeDtypeStruct((length, wide), BF16),
        ],
        compiler_params=pltpu.CompilerParams(vmem_limit_bytes=48 * 2**20),
        cost_estimate=pl.CostEstimate(
            flops=20 * 10**9, bytes_accessed=6 * 2**20, transcendentals=5 * 10**6
        ),
        name=f"attend_backward_{pair}",
    )(place, slopes, queries_t, keys, values, grads_t, full, logs)


def swap(value, axis, distance):
    size = lax.axis_size(axis)
    return lax.ppermute(value, axis, [(i, i ^ distance) for i in range(size)])


def after(value, *earlier):
    return lax.optimization_barrier((value,) + earlier)[0]


def exchange_blocks(parts):
    return [parts[0]] + [swap(parts[j], "tensor", j) for j in range(1, 4)]


def chip_sum(far, far_near):
    return add_rows(far, swap(far_near, "tensor", 1))


def add_rows(one, two):
    rows, width = two.shape
    tile = rows // 2
    block = pl.BlockSpec((tile, width), lambda i: (i, 0))

    def add(one_ref, two_ref, out_ref):
        out_ref[...] = (one_ref[...].astype(F32) + two_ref[...].astype(F32)).astype(BF16)

    return pl.pallas_call(
        add,
        grid=(2,),
        in_specs=[block, block],
        out_specs=block,
        out_shape=jax.ShapeDtypeStruct((rows, width), BF16),
        compiler_params=pltpu.CompilerParams(vmem_limit_bytes=32 * 2**20),
        cost_estimate=pl.CostEstimate(
            flops=rows * width, bytes_accessed=6 * rows * width, transcendentals=0
        ),
        name="add_rows",
    )(one, two)


def sum_over(value, axes, *earlier):
    for axis in axes:
        size = lax.axis_size(axis)
        distance = 1
        while distance < size:
            if distance * 4 <= size:
                one, two, three = (swap(value, axis, distance * k) for k in (1, 2, 3))
                value = after((value + one) + (two + three), *earlier)
                distance *= 4
            else:
                value = value + swap(value, axis, distance)
                distance *= 2
    return value


def ring_dp():
    count = lax.axis_size("dp")
    return list(range(0, count, 2)) + list(range(count - 1, 0, -2))


def gather_dp(shard):
    return lax.all_gather(shard, "dp", axis=0, tiled=True, axis_index_groups=[ring_dp()])


def scatter_dp(blocks):
    return lax.psum_scatter(
        blocks, "dp", scatter_dimension=0, tiled=True, axis_index_groups=[ring_dp()]
    ).astype(F32)


def at_ring(place, count):
    return jnp.where(place < count // 2, 2 * place, 2 * (count - 1 - place) + 1)


def place_in_ring(owner, count):
    return jnp.where(owner % 2 == 0, owner // 2, count - 1 - owner // 2)


def reorder(blocks, order, name):
    count = lax.axis_size("dp")
    rows, width = blocks.shape[0] // count, blocks.shape[1]

    def copy(source_ref, result_ref):
        result_ref[...] = source_ref[...]

    return pl.pallas_call(
        copy,
        grid=(count,),
        in_specs=[pl.BlockSpec((rows, width), lambda i: (order(i, count), 0))],
        out_specs=pl.BlockSpec((rows, width), lambda i: (i, 0)),
        out_shape=jax.ShapeDtypeStruct(blocks.shape, blocks.dtype),
        cost_estimate=pl.CostEstimate(
            flops=0, bytes_accessed=4 * count * rows * width, transcendentals=0
        ),
        name=name,
    )(blocks)


def ring_lanes(rows, width, index=0):
    count = lax.axis_size("dp")
    lanes = width // count
    if lanes % 128:
        return [pl.BlockSpec((rows, 256), lambda i: (index, i))]
    return [
        pl.BlockSpec((rows, lanes), lambda i, k=k: (index, at_ring(2 * i + k, count)))
        for k in range(2)
    ]


def project_kernel(ring, *refs):
    blocks, refs = refs[:4], refs[4:]
    weight_ref, bias_ref, q_ref, k_ref, v_ref, full_ref = refs
    width = q_ref.shape[0]
    step = pl.program_id(0)

    @pl.when(step == 0)
    def _():
        rows = full_ref.shape[0] // len(ring)
        for at, owner in enumerate(ring):
            full_ref[owner * rows : (owner + 1) * rows, :] = weight_ref[at * rows : (at + 1) * rows, :]

    for k, block in enumerate(blocks):

        @pl.when(step == k)
        def _(block=block):
            out = jnp.dot(block[...], full_ref[:, : 3 * width], preferred_element_type=F32)
            q_ref[...] = (out[:, :width] + bias_ref[0:1, :]).astype(BF16).T
            k_ref[...] = out[:, width : 2 * width].astype(BF16)
            v_ref[...] = (out[:, 2 * width :] + bias_ref[1:2, :]).astype(BF16)


def project(blocks, weights, bias):
    rows = blocks[0].shape[0]
    width = bias.shape[1]
    count = len(blocks)
    ring = ring_dp()

    def whole(shape):
        return pl.BlockSpec(shape, lambda i: (0, 0))

    return pl.pallas_call(
        functools.partial(project_kernel, ring),
        grid=(count,),
        in_specs=[whole(b.shape) for b in blocks] + [whole(weights.shape), whole(bias.shape)],
        out_specs=[
            pl.BlockSpec((width, rows), lambda i: (0, i)),
            pl.BlockSpec((rows, width), lambda i: (i, 0)),
            pl.BlockSpec((rows, width), lambda i: (i, 0)),
            whole(weights.shape),
        ],
        out_shape=[
            jax.ShapeDtypeStruct((width, count * rows), BF16),
            jax.ShapeDtypeStruct((count * rows, width), BF16),
            jax.ShapeDtypeStruct((count * rows, width), BF16),
            jax.ShapeDtypeStruct(weights.shape, BF16),
        ],
        compiler_params=pltpu.CompilerParams(vmem_limit_bytes=40 * 2**20),
        cost_estimate=pl.CostEstimate(
            flops=6 * count * rows * width * weights.shape[0],
            bytes_accessed=12 * 2**20,
            transcendentals=0,
        ),
        name="project",
    )(*blocks, weights, bias)


def in_ring(blocks, width, name):
    if (width // lax.axis_size("dp")) % 128:
        return reorder(blocks, at_ring, name)
    return blocks


def rows_of(value, count):
    size = value.shape[0] // count
    return [value[i * size : (i + 1) * size] for i in range(count)]


def dot(a, b, ca, cb):
    return lax.dot_general(a, b, (((ca,), (cb,)), ((), ())), preferred_element_type=F32)


def body(
    hidden_in,
    norm_gain,
    norm_shift,
    qkv_weight,
    qv_bias,
    out_weight,
    out_bias,
    up_weight,
    up_bias,
    down_weight,
    cotangent,
):
    rows, width = hidden_in.shape
    tensor_size = lax.axis_size("tensor")
    heads_wide = qkv_weight.shape[2]
    hidden_units = up_weight.shape[1]
    local_heads = HEADS // tensor_size
    head_dim = heads_wide // local_heads
    pairs = local_heads // 2
    wide = 2 * head_dim
    me = lax.axis_index("tensor").astype(jnp.int32)
    place = me.reshape(1)
    head_ids = me * local_heads + jnp.arange(local_heads, dtype=jnp.int32)
    slopes = jnp.exp2(-8.0 * (head_ids.astype(F32) + 1.0) / HEADS) * LOG2E
    part = rows // 2
    stat = functools.partial(row_call, rows=rows, width=width)
    row_f32 = jax.ShapeDtypeStruct((rows, width), F32)
    row_bf16 = jax.ShapeDtypeStruct((rows, width), BF16)
    part_bf16 = jax.ShapeDtypeStruct((part, width), BF16)
    four_f32 = jax.ShapeDtypeStruct((4, width), F32)

    first_shard = jnp.concatenate(
        [qkv_weight[0], qkv_weight[1], qkv_weight[2], out_weight.T], axis=1
    )
    second_shard = jnp.concatenate([up_weight, down_weight.T], axis=1)
    first_ring = gather_dp(first_shard)
    second_weights = gather_dp(second_shard)

    (normed,) = stat(
        first_norm_kernel, arrays=[hidden_in, norm_gain, norm_shift], outs=[row_bf16], name="norm_one"
    )
    normed_far = swap(normed, "tensor", 2)
    normed_near = swap(normed, "tensor", 1)
    normed_blocks = [normed, normed_near, normed_far, swap(normed_far, "tensor", 1)]
    grads_far = swap(cotangent, "tensor", 2)
    grads_near = swap(cotangent, "tensor", 1)
    grads_far_near = swap(grads_far, "tensor", 1)

    queries_t, keys, values, first_full = project(normed_blocks, first_ring, qv_bias)
    out_mine = first_full[:, 3 * heads_wide :]
    out_far = swap(out_mine, "tensor", 2)
    kept = []
    mixed_parts = [[] for _ in range(tensor_size)]
    received = out_far
    for pair in range(pairs):
        mixed_t, mixed_full, logs = attend_forward(
            place,
            slopes,
            queries_t
            if pair == 0
            else after(queries_t, grads_far, mixed_full),
            keys,
            values,
            rows,
            head_dim,
            pair,
        )
        if pair > 0:
            mixed_t = after(mixed_t, *received, out_far)
        kept.append((mixed_full, logs))
        parts = [mixed_t[:, j * rows : (j + 1) * rows] for j in range(tensor_size)]
        received = exchange_blocks(parts)
        for j, block in enumerate(received):
            mixed_parts[j].append(block)
    out_full = jnp.concatenate(
        [out_mine, swap(out_mine, "tensor", 1), out_far, swap(out_far, "tensor", 1)], axis=1
    )
    mixed_all = jnp.concatenate([block for group in mixed_parts for block in group], axis=0)
    attn_sum = dot(mixed_all, out_full, 0, 1)
    middle, second = stat(
        second_norm_kernel,
        arrays=[hidden_in, attn_sum, out_bias, norm_gain, norm_shift],
        outs=[row_f32, (part_bf16, part_bf16)],
        name="norm_two",
    )

    up_bias_row = up_bias.reshape(1, hidden_units)
    far_chunks = [swap(second[c], "tensor", 2) for c in range(2)]
    seconds = [[(block, 0) for block in second]]
    seconds[0] += [(swap(block, "tensor", 1), 0) for block in second]
    grads = [[(g, c) for g in (cotangent, grads_near) for c in range(2)]]
    mlp_a, back_a, active, upper, sums_up = feed(
        part, seconds[0], grads[0], second_weights, up_bias_row, jnp.zeros_like(up_bias_row), "feed_near"
    )
    actives, uppers = [active], [upper]
    mlps, back_fars = [], []
    earlier = (mlp_a[0],)
    for c in range(2):
        far = after(far_chunks[c], *earlier)
        pair_c = [(far, 0), (swap(far, "tensor", 1), 0)]
        if c > 0:
            pair_c[0] = (after(far, mine), 0)
        grads_c = [(grads_far, c), (grads_far_near, c)]
        mlp_c, back_c, active, upper, sums_up = feed(
            part, pair_c, grads_c, second_weights, up_bias_row, sums_up, f"feed_far_{c}"
        )
        earlier = (mlp_c[0],)
        seconds.append(pair_c)
        grads.append(grads_c)
        actives.append(active)
        uppers.append(upper)
        mlps.append(mlp_c)
        mine = chip_sum(back_c[0], after(back_c[1], *back_fars))
        back_fars.append(swap(mine, "tensor", 2))
    back_near = tuple(swap(back_a[2 + c], "tensor", 1) for c in range(2))

    uppers[0] = after(uppers[0], back_fars[0], mine)
    grad_second_w = weight_grads(part, seconds, grads, uppers, actives)
    local_second_w = grad_second_w
    grad_second_w = scatter_dp(grad_second_w)
    grad_up_weight = grad_second_w[:, :hidden_units]
    grad_down_weight = grad_second_w[:, hidden_units:].T

    grad_middle, grad_attn, early = stat(
        second_back_kernel,
        arrays=[after(middle, local_second_w), cotangent, tuple(back_a[:2]), back_near, tuple(back_fars), norm_gain],
        outs=[row_f32, row_bf16, four_f32],
        name="norm_two_back",
    )
    mixed_grads = dot(out_full, grad_attn, 0, 1).astype(BF16)
    mlps = [lax.optimization_barrier((*m, grad_attn))[:2] for m in mlps]
    mlp_a = lax.optimization_barrier((*mlp_a, grad_attn))[:4]
    exchanged = exchange_blocks(rows_of(mixed_grads, tensor_size))
    grads_t = [
        jnp.concatenate([block[pair * wide : (pair + 1) * wide] for block in exchanged], axis=1)
        for pair in range(pairs)
    ]

    out_partial = dot(after(grad_attn, mixed_grads), mixed_all, 0, 1).astype(BF16)
    out_cols = [out_partial[:, j * heads_wide : (j + 1) * heads_wide] for j in range(tensor_size)]
    out_mine_sum = chip_sum(out_cols[2], out_cols[3])
    mlp_mine_sum = jnp.concatenate([chip_sum(m[0], m[1]) for m in mlps], axis=0)
    mlp_far = swap(mlp_mine_sum, "tensor", 2)
    out_near = swap(out_cols[1], "tensor", 1)
    out_far_sum = swap(after(out_mine_sum, mlp_far), "tensor", 2)
    mlp_near = tuple(swap(m, "tensor", 1) for m in mlp_a[2:])
    low = []
    for pair in range(pairs):
        grads_pair = grads_t[pair]
        if pair == 0:
            grads_pair = after(grads_pair, out_mine_sum, mlp_mine_sum)
        else:
            grads_pair = after(grads_pair, low[-1][0], mlp_far)
        mixed_full, logs = kept[pair]
        low.append(
            attend_backward(
                place, slopes, queries_t, keys, values, grads_pair, mixed_full, logs, rows, head_dim, pair
            )
        )
    low[-1] = lax.optimization_barrier((*low[-1], out_far_sum))[:3]
    out_sum = (
        out_cols[0].astype(F32) + out_near.astype(F32) + out_far_sum.astype(F32)
    ).astype(BF16)
    joined, column_sums = join_low(low)
    first_cols = first_full[:, : 3 * heads_wide]
    half = 2 * rows
    far_grads = dot(joined[half:], first_cols, 1, 1).astype(BF16)
    first_mine = add_rows(far_grads, swap(far_grads[rows:], "tensor", 1))
    first_far = swap(first_mine, "tensor", 2)
    send, gains = first_grads(
        normed_blocks, after(joined, first_mine), column_sums, out_sum, first_ring
    )
    first_sums = scatter_dp(after(send, grad_second_w))
    near_grads = dot(after(joined, send)[:half], first_cols, 1, 1).astype(BF16)
    first_near = swap(near_grads[rows:], "tensor", 1)

    grad_qkv = jnp.stack([first_sums[:, c * heads_wide : (c + 1) * heads_wide] for c in range(3)])
    grad_out_weight = first_sums[:, 3 * heads_wide :].T

    (grad_in,) = stat(
        first_back_kernel,
        arrays=[hidden_in, grad_middle, near_grads[:rows], first_near, first_far, norm_gain],
        outs=[row_f32],
        name="norm_one_back",
    )
    (block_out,) = stat(
        block_kernel,
        arrays=[middle, tuple(mlp_a[:2]), mlp_near, after(mlp_far, near_grads), out_bias],
        outs=[row_f32],
        name="block_out",
    )

    shift_sum = gains[:, 1]
    gain_sum = (gains[:, 0] - norm_shift[0] * shift_sum) / norm_gain[0]
    lanes = 128
    whole_sums = jnp.concatenate([early, gain_sum[None], shift_sum[None]], axis=0).reshape(-1, lanes)
    columns = column_sums[0]
    split_sums = jnp.concatenate(
        [columns[:heads_wide], columns[2 * heads_wide :], sums_up[0]]
    ).reshape(-1, lanes)
    sums = sum_over(jnp.concatenate([whole_sums, split_sums], axis=0), ("dp",), first_far, block_out, grad_up_weight, grad_down_weight)
    whole_sums = sum_over(sums[: whole_sums.shape[0]], ("tensor",)).reshape(-1, width)
    split_sums = sums[whole_sums.size // lanes :].reshape(-1)
    return (
        block_out,
        grad_in,
        jnp.stack([whole_sums[4], whole_sums[0]]),
        jnp.stack([whole_sums[5], whole_sums[1]]),
        grad_qkv,
        split_sums[: 2 * heads_wide].reshape(2, heads_wide),
        grad_out_weight,
        whole_sums[2:4],
        grad_up_weight,
        split_sums[2 * heads_wide :],
        grad_down_weight,
    )


def solution(mesh):
    return jax.shard_map(
        body,
        mesh=mesh,
        in_specs=(
            P(("dp", "tensor"), None),
            P(),
            P(),
            P(None, "dp", "tensor"),
            P(None, "tensor"),
            P("tensor", "dp"),
            P(),
            P("dp", "tensor"),
            P("tensor"),
            P("tensor", "dp"),
            P(("dp", "tensor"), None),
        ),
        out_specs=(
            P(("dp", "tensor"), None),
            P(("dp", "tensor"), None),
            P(),
            P(),
            P(None, "dp", "tensor"),
            P(None, "tensor"),
            P("tensor", "dp"),
            P(),
            P("dp", "tensor"),
            P("tensor"),
            P("tensor", "dp"),
        ),
        check_vma=False,
    )
```

```python
import functools
import math

import jax
import jax.numpy as jnp
from jax import lax
from jax.experimental import pallas as pl
from jax.experimental.pallas import tpu as pltpu
from jax.sharding import PartitionSpec as P

HEADS = 16
LOG2E = 1.4426950408889634
NEG = -1e30
BF16 = jnp.bfloat16
F32 = jnp.float32


def normalise(values):
    average = jnp.mean(values, axis=-1, keepdims=True)
    centered = values - average
    inverse = lax.rsqrt(jnp.mean(centered * centered, axis=-1, keepdims=True) + 1e-05)
    return centered * inverse, inverse


def gelu_both(values):
    first = 0.7978845608
    square = values * values
    tangent = jnp.tanh(values * (first + (first * 0.044715) * square))
    half = 0.5 + 0.5 * tangent
    active = values * half
    slope = half + (values - values * (tangent * tangent)) * (
        0.5 * first + (1.5 * 0.044715 * first) * square
    )
    return active, slope


def first_norm_kernel(hidden, gain, shift, put_normed):
    scaled, _ = normalise(hidden().astype(F32))
    put_normed((scaled * gain()[0:1, :] + shift()[0:1, :]).astype(BF16))


def second_norm_kernel(hidden, attn, bias, gain, shift, put_middle, put_normed):
    middle = hidden().astype(F32) + attn() + bias()[0:1, :]
    put_middle(middle)
    scaled, _ = normalise(middle)
    put_normed((scaled * gain()[1:2, :] + shift()[1:2, :]).astype(BF16))


def back_of_norm(value, own, near, far, gain):
    scaled, inverse = normalise(value.astype(F32))
    gradient = own.astype(F32) + near.astype(F32) + far.astype(F32)
    grad_scaled = gradient * gain
    grad_mean = jnp.mean(grad_scaled, axis=-1, keepdims=True)
    grad_proj = jnp.mean(grad_scaled * scaled, axis=-1, keepdims=True)
    return inverse * (grad_scaled - grad_mean - scaled * grad_proj), gradient, scaled


def second_back_kernel(middle, above, own, near, far, gain, put_total, put_low, add_sums):
    change, gradient, scaled = back_of_norm(middle(), own(), near(), far(), gain()[1:2, :])
    grads = above().astype(F32)
    total = grads + change
    put_total(total)
    put_low(total.astype(BF16))
    columns = [gradient * scaled, gradient, total, grads]
    add_sums(jnp.concatenate([jnp.sum(c, axis=0, keepdims=True) for c in columns], axis=0))


def first_back_kernel(hidden, above, own, near, far, gain, put_total):
    change, _, _ = back_of_norm(hidden(), own(), near(), far(), gain()[0:1, :])
    put_total(above() + change)


def block_kernel(middle, own, near, far, bias, put_block):
    mlp = own().astype(F32) + near().astype(F32) + far().astype(F32)
    put_block(middle() + mlp + bias()[1:2, :])


def row_call(kernel, rows, width, arrays, outs, name, tile=256):
    tile = min(tile, rows // 2)
    half = rows // 2 // tile

    def specs(array):
        if isinstance(array, tuple):
            return [
                pl.BlockSpec((tile, width), lambda i: (jnp.minimum(i, half - 1), 0)),
                pl.BlockSpec((tile, width), lambda i: (jnp.maximum(i - half, 0), 0)),
            ]
        if array.shape[0] == rows:
            return [pl.BlockSpec((tile, width), lambda i: (i, 0))]
        return [pl.BlockSpec(array.shape, lambda i: (0, 0))]

    def flat(values):
        return [v for value in values for v in (value if isinstance(value, tuple) else (value,))]

    def run(*refs):
        step = pl.program_id(0)
        at = 0
        accesses = []
        for k, value in enumerate(arrays + outs):
            reads = k < len(arrays)
            if isinstance(value, tuple):
                one, two = refs[at : at + 2]
                at += 2
                if reads:
                    accesses.append(lambda a=one, b=two: jnp.where(step < half, a[...], b[...]))
                else:

                    def put(block, a=one, b=two):
                        @pl.when(step < half)
                        def _():
                            a[...] = block

                        @pl.when(step >= half)
                        def _():
                            b[...] = block

                    accesses.append(put)
                continue
            ref = refs[at]
            at += 1
            if reads:
                accesses.append(lambda a=ref: a[...])
            elif value.shape[0] == rows:

                def put(block, a=ref):
                    a[...] = block

                accesses.append(put)
            else:

                def add(block, a=ref):
                    @pl.when(step == 0)
                    def _():
                        a[...] = block

                    @pl.when(step > 0)
                    def _():
                        a[...] += block

                accesses.append(add)
        kernel(*accesses)

    results = pl.pallas_call(
        run,
        grid=(2 * half,),
        in_specs=[spec for a in arrays for spec in specs(a)],
        out_specs=[spec for o in outs for spec in specs(o)],
        out_shape=flat(outs),
        compiler_params=pltpu.CompilerParams(vmem_limit_bytes=32 * 2**20),
        cost_estimate=pl.CostEstimate(
            flops=20 * rows * width, bytes_accessed=12 * rows * width, transcendentals=rows
        ),
        name=name,
    )(*flat(arrays))
    results = list(results)
    return [
        (results.pop(0), results.pop(0)) if isinstance(o, tuple) else results.pop(0) for o in outs
    ]


def feed_kernel(count, ring, *refs):
    seconds, grads = refs[:count], refs[count : 2 * count]
    bias_ref, before_ref = refs[2 * count : 2 * count + 2]
    parts, refs = refs[2 * count + 2], refs[2 * count + 3 :]
    mlps, backs = refs[:count], refs[count : 2 * count]
    active_ref, upper_ref, sums_ref, weight_ref, arrived = refs[2 * count :]
    hidden = bias_ref.shape[1]
    up_ref, down_ref = weight_ref.at[:, :hidden], weight_ref.at[:, hidden:]
    step = pl.program_id(0)
    contract = (((1,), (1,)), ((), ()))

    @pl.when(step == 0)
    def _():
        sums_ref[...] = before_ref[...]
        rows = parts.shape[0] // len(ring)
        copies = [
            pltpu.make_async_copy(
                parts.at[at * rows : (at + 1) * rows, :],
                weight_ref.at[owner * rows : (owner + 1) * rows, :],
                arrived.at[at],
            )
            for at, owner in enumerate(ring)
        ]
        for copy in copies:
            copy.start()
        for copy in copies:
            copy.wait()

    for k in range(count):

        @pl.when(step == k)
        def _(k=k):
            upper = jnp.dot(seconds[k][...], up_ref[...], preferred_element_type=F32) + bias_ref[...]
            active, slope = gelu_both(upper)
            active = active.astype(BF16)
            active_ref[...] = active
            grad_active = jnp.dot(grads[k][...], down_ref[...], preferred_element_type=F32)
            grad_upper = (grad_active * slope).astype(BF16)
            upper_ref[...] = grad_upper
            backs[k][...] = lax.dot_general(
                grad_upper, up_ref[...], contract, preferred_element_type=F32
            ).astype(BF16)
            mlps[k][...] = lax.dot_general(
                active, down_ref[...], contract, preferred_element_type=F32
            ).astype(BF16)
            sums_ref[...] += jnp.sum(grad_upper.astype(F32), axis=0, keepdims=True)


def feed(tile, seconds, grads, weights, bias, before, name):
    count, ring = len(seconds), ring_dp()
    width = seconds[0][0].shape[1]
    hidden = bias.shape[1]
    block = pl.BlockSpec((tile, width), lambda i: (0, 0))

    def at(k):
        return pl.BlockSpec((tile, width), lambda i: (k, 0))

    by_hidden = pl.BlockSpec((tile, hidden), lambda i: (i, 0))
    row = pl.BlockSpec((1, hidden), lambda i: (0, 0))
    results = pl.pallas_call(
        functools.partial(feed_kernel, count, ring),
        grid=(count,),
        in_specs=[at(k) for _, k in seconds + grads]
        + [row, row, pl.BlockSpec(memory_space=pl.ANY)],
        out_specs=[block] * (2 * count) + [by_hidden, by_hidden, row],
        scratch_shapes=[
            pltpu.VMEM((width, 2 * hidden), BF16),
            pltpu.SemaphoreType.DMA((len(ring),)),
        ],
        out_shape=[jax.ShapeDtypeStruct((tile, width), BF16)] * (2 * count)
        + [
            jax.ShapeDtypeStruct((count * tile, hidden), BF16),
            jax.ShapeDtypeStruct((count * tile, hidden), BF16),
            jax.ShapeDtypeStruct((1, hidden), F32),
        ],
        compiler_params=pltpu.CompilerParams(vmem_limit_bytes=36 * 2**20),
        cost_estimate=pl.CostEstimate(
            flops=8 * count * tile * width * hidden,
            bytes_accessed=16 * 2**20,
            transcendentals=count * tile * hidden,
        ),
        name=name,
    )(*(a for a, _ in seconds + grads), bias, before, weights)
    return results[:count], results[count : 2 * count], results[-3], results[-2], results[-1]


def weight_kernel(groups, split, *refs):
    out_ref = refs[-1]
    blocks = sum(groups) * split
    rights = refs[2 * blocks : -1]
    hidden = rights[0].shape[1]
    for side in range(2):
        lefts = refs[side * blocks : (side + 1) * blocks]
        total = None
        at = 0
        for g, count in enumerate(groups):
            rows = [
                jnp.concatenate([r[...] for r in lefts[at + k * split : at + (k + 1) * split]], axis=1)
                for k in range(count)
            ]
            at += count * split
            term = lax.dot_general(
                jnp.concatenate(rows, axis=0),
                rights[side * len(groups) + g][...],
                (((0,), (0,)), ((), ())),
                preferred_element_type=F32,
            )
            total = term if total is None else total + term
        out_ref[:, side * hidden : (side + 1) * hidden] = total.astype(BF16)


def weight_grads(rows, seconds, grads, uppers, actives):
    groups = [len(g) for g in seconds]
    lefts = [b for g in seconds for b in g] + [b for g in grads for b in g]
    width = lefts[0][0].shape[1]
    hidden = uppers[0].shape[1]
    specs = [(a, spec) for a, k in lefts for spec in ring_lanes(rows, width, k)]
    split = len(specs) // len(lefts)
    result = pl.pallas_call(
        functools.partial(weight_kernel, groups, split),
        grid=(width // 256,),
        in_specs=[spec for _, spec in specs]
        + [pl.BlockSpec(r.shape, lambda i: (0, 0)) for r in uppers + actives],
        out_specs=pl.BlockSpec((256, 2 * hidden), lambda i: (i, 0)),
        out_shape=jax.ShapeDtypeStruct((width, 2 * hidden), BF16),
        compiler_params=pltpu.CompilerParams(vmem_limit_bytes=36 * 2**20),
        cost_estimate=pl.CostEstimate(
            flops=2 * len(lefts) * rows * width * hidden,
            bytes_accessed=20 * 2**20,
            transcendentals=0,
        ),
        name="weight_grads",
    )(*(a for a, _ in specs), *uppers, *actives)
    return in_ring(result, width, "weight_order")


def join_kernel(pairs, *refs):
    lows, (joined_ref, sums_ref) = refs[: 3 * pairs], refs[3 * pairs :]
    wide = lows[0].shape[0]
    for c in range(3):
        for pair in range(pairs):
            low = lows[3 * pair + c][...]
            at = (c * pairs + pair) * wide
            joined_ref[:, at : at + wide] = low.T if c == 0 else low
    sums = jnp.sum(joined_ref[...].astype(F32), axis=0, keepdims=True)

    @pl.when(pl.program_id(0) == 0)
    def _():
        sums_ref[...] = sums

    @pl.when(pl.program_id(0) > 0)
    def _():
        sums_ref[...] += sums


def join_low(low):
    pairs = len(low)
    wide, length = low[0][0].shape
    lanes = 3 * pairs * wide
    tile = min(512, length)
    specs = [
        pl.BlockSpec((wide, tile), lambda i: (0, i)),
        pl.BlockSpec((tile, wide), lambda i: (i, 0)),
        pl.BlockSpec((tile, wide), lambda i: (i, 0)),
    ]
    return pl.pallas_call(
        functools.partial(join_kernel, pairs),
        grid=(length // tile,),
        in_specs=specs * pairs,
        out_specs=[
            pl.BlockSpec((tile, lanes), lambda i: (i, 0)),
            pl.BlockSpec((1, lanes), lambda i: (0, 0)),
        ],
        out_shape=[
            jax.ShapeDtypeStruct((length, lanes), BF16),
            jax.ShapeDtypeStruct((1, lanes), F32),
        ],
        compiler_params=pltpu.CompilerParams(vmem_limit_bytes=32 * 2**20),
        cost_estimate=pl.CostEstimate(
            flops=length * lanes, bytes_accessed=4 * length * lanes, transcendentals=0
        ),
        name="join_low",
    )(*(g for group in low for g in group))


def first_kernel(blocks, split, *refs):
    lefts, refs = refs[: blocks * split], refs[blocks * split :]
    outs, (right_ref, sums_ref, weight_ref, grad_ref, gain_ref) = refs[:split], refs[split:]
    left = jnp.concatenate(
        [
            jnp.concatenate([r[...] for r in lefts[k * split : (k + 1) * split]], axis=1)
            for k in range(blocks)
        ],
        axis=0,
    )
    grads = lax.dot_general(
        left, right_ref[...], (((0,), (0,)), ((), ())), preferred_element_type=F32
    )
    width = grads.shape[1]
    grad_ref[:, :width] = grads.astype(BF16)
    grad_ref[:, width:] = jnp.concatenate([r[...] for r in outs], axis=0)
    weight = weight_ref[:, :width].astype(F32)
    gain = jnp.sum(weight * grads, axis=1, keepdims=True)
    shift = jnp.sum(weight * sums_ref[...], axis=1, keepdims=True)
    lane = lax.broadcasted_iota(jnp.int32, gain_ref.shape, 1)
    gain_ref[...] = jnp.where(lane == 0, gain, shift)


def first_grads(normed_blocks, joined, sums, out_sum, weights):
    rows, width = normed_blocks[0].shape
    length, lanes = joined.shape
    count = lax.axis_size("dp")
    out_wide = out_sum.shape[1]
    lefts = ring_lanes(rows, width)
    split = len(lefts)
    if split == 1:
        outs = [pl.BlockSpec((256, out_wide), lambda i: (i, 0))]
        weights = reorder(weights, place_in_ring, "first_order")
    else:
        outs = [
            pl.BlockSpec((width // count, out_wide), lambda i, k=k: (at_ring(2 * i + k, count), 0))
            for k in range(2)
        ]

    def whole(shape):
        return pl.BlockSpec(shape, lambda i: (0, 0))

    grads, gains = pl.pallas_call(
        functools.partial(first_kernel, len(normed_blocks), split),
        grid=(width // 256,),
        in_specs=lefts * len(normed_blocks)
        + outs
        + [
            whole(joined.shape),
            whole(sums.shape),
            pl.BlockSpec((256, weights.shape[1]), lambda i: (i, 0)),
        ],
        out_specs=[
            pl.BlockSpec((256, lanes + out_wide), lambda i: (i, 0)),
            pl.BlockSpec((256, 128), lambda i: (i, 0)),
        ],
        out_shape=[
            jax.ShapeDtypeStruct((width, lanes + out_wide), BF16),
            jax.ShapeDtypeStruct((width, 128), F32),
        ],
        compiler_params=pltpu.CompilerParams(vmem_limit_bytes=50 * 2**20),
        cost_estimate=pl.CostEstimate(
            flops=2 * length * width * lanes, bytes_accessed=12 * 2**20, transcendentals=0
        ),
        name="first_grads",
    )(
        *(b for block in normed_blocks for b in [block] * split),
        *[out_sum] * split,
        joined,
        sums,
        weights,
    )
    gains = gains[:, :2]
    if split == 1:
        return reorder(grads, at_ring, "first_grad_order"), gains
    ring = ring_dp()
    parts = rows_of(gains, count)
    return grads, jnp.concatenate([parts[ring.index(k)] for k in range(count)], axis=0)


def fill_bias(bias, masked, slope):
    size = bias.shape[0]
    key = lax.broadcasted_iota(jnp.int32, (size, size), 0)
    query = lax.broadcasted_iota(jnp.int32, (size, size), 1)
    value = key.astype(F32) * slope
    bias[...] = value
    masked[...] = jnp.where(key <= query, value, NEG)


def head_rows(block, head):
    half = block.shape[0] // 2
    rows = lax.broadcasted_iota(jnp.int32, block.shape, 0)
    keep = (rows < half) if head == 0 else (rows >= half)
    return jnp.where(keep, block, jnp.zeros_like(block))


def forward_kernel(
    place, slope_ref, q_ref, k_ref, v_ref, mixed_ref, full_ref, log_ref, bias, masked, values_t, *, scale, pair
):
    query_block = pl.program_id(0)
    me = place[0]
    size = bias.shape[1]
    half = q_ref.shape[0] // 2

    @pl.when(query_block == 0)
    def _():
        values_t[...] = v_ref[...].T
        for head in range(2):
            fill_bias(bias.at[head], masked.at[head], slope_ref[2 * pair + head])

    outputs = []
    logs = []
    for head in range(2):
        step = slope_ref[2 * pair + head] * size
        queries = head_rows(q_ref[...], head)

        def block(key_block, carry, bias_block, queries, count=size, head=head, step=step):
            top, total, acc = carry
            at = pl.multiple_of((key_block ^ me) * size, size)
            raw = jnp.dot(k_ref[pl.ds(at, count), :], queries, preferred_element_type=F32)
            scores = raw * scale + bias_block
            base = key_block.astype(F32) * step
            new_top = jnp.maximum(top, jnp.max(scores, axis=0, keepdims=True) + base)
            weights = jnp.exp2(scores - (new_top - base))
            fade = jnp.exp2(top - new_top)
            total = total * fade + jnp.sum(weights, axis=0, keepdims=True)
            rows = values_t[head * half : (head + 1) * half, pl.ds(at, count)]
            acc = acc * fade + jnp.dot(rows, weights.astype(BF16), preferred_element_type=F32)
            return new_top, total, acc

        start = (
            jnp.full((1, size), NEG, F32),
            jnp.zeros((1, size), F32),
            jnp.zeros((half, size), F32),
        )
        carry = lax.fori_loop(
            0,
            query_block,
            lambda i, c, head=head, block=block, queries=queries: block(i, c, bias[head], queries),
            start,
        )
        middle = size // 2
        one = block(
            query_block,
            tuple(c[:, :middle] for c in carry),
            masked[head, :middle, :middle],
            queries[:, :middle],
            middle,
        )
        two = block(
            query_block,
            tuple(c[:, middle:] for c in carry),
            masked[head, :, middle:],
            queries[:, middle:],
        )
        top, total, acc = (jnp.concatenate(c, axis=1) for c in zip(one, two))
        outputs.append(acc / total)
        logs.append(top + jnp.log2(total))
    result = jnp.concatenate(outputs, axis=0)
    full_ref[...] = result
    mixed_ref[...] = result.astype(BF16)
    log_ref[...] = jnp.concatenate(logs, axis=0)


def backward_kernel(
    place,
    slope_ref,
    q_ref,
    k_ref,
    v_ref,
    g_ref,
    full_ref,
    log_ref,
    gq_ref,
    gk_ref,
    gv_ref,
    bias,
    masked,
    gq_acc,
    delta,
    *,
    scale,
    factor,
    pair,
):
    key_block = pl.program_id(0)
    blocks = pl.num_programs(0)
    me = place[0]
    size = bias.shape[1]
    half = q_ref.shape[0] // 2

    @pl.when(key_block == 0)
    def _():
        gq_acc[...] = jnp.zeros_like(gq_acc)
        for head in range(2):
            fill_bias(bias.at[head], masked.at[head], slope_ref[2 * pair + head])
            rows = slice(head * half, (head + 1) * half)
            delta[head : head + 1, :] = jnp.sum(
                g_ref[rows, :].astype(F32) * full_ref[rows, :], axis=0, keepdims=True
            )

    keys = k_ref[...]
    keys_t = keys.T
    values = v_ref[...]
    grad_k = jnp.zeros(keys.shape, F32)
    grad_v = jnp.zeros(keys.shape, F32)
    for head in range(2):
        base = key_block.astype(F32) * (slope_ref[2 * pair + head] * size)
        rows = slice(head * half, (head + 1) * half)

        def block(query_block, carry, bias_block, skip, count, head=head, base=base, rows=rows):
            grad_k, grad_v = carry
            seen, wide = bias_block.shape
            at = pl.multiple_of((query_block ^ me) * size + skip, size if skip == 0 else skip)
            queries = head_rows(q_ref[:, pl.ds(at, wide)], head)
            grads = head_rows(g_ref[:, pl.ds(at, wide)], head)
            raw = jnp.dot(keys[:seen], queries, preferred_element_type=F32)
            log = log_ref[head : head + 1, pl.ds(at, wide)] - base
            weights = jnp.exp2(raw * scale + (bias_block - log))
            along = jnp.dot(values[:seen], grads, preferred_element_type=F32)
            change = (weights * (along - delta[head : head + 1, pl.ds(at, wide)])).astype(BF16)
            contract = (((1,), (1,)), ((), ()))
            more_v = lax.dot_general(
                weights.astype(BF16), grads, contract, preferred_element_type=F32
            )
            more_k = lax.dot_general(change, queries, contract, preferred_element_type=F32)
            gq_acc[rows, pl.ds(at, wide)] += jnp.dot(
                keys_t[rows, :seen], change, preferred_element_type=F32
            )
            if seen == count:
                return grad_k + more_k, grad_v + more_v
            return tuple(
                jnp.concatenate([g[:seen] + m, g[seen:]], axis=0)
                for g, m in ((grad_k, more_k), (grad_v, more_v))
            )

        middle = size // 2
        carry = block(key_block, (grad_k, grad_v), masked[head, :middle, :middle], 0, size)
        carry = block(key_block, carry, masked[head, :, middle:], middle, size)
        grad_k, grad_v = lax.fori_loop(
            key_block + 1,
            blocks,
            lambda i, c, head=head, block=block: block(i, c, bias[head], 0, size),
            carry,
        )
    low_k = (grad_k * factor).astype(BF16)
    low_v = grad_v.astype(BF16)
    gk_ref[...] = low_k
    gv_ref[...] = low_v

    @pl.when(key_block == blocks - 1)
    def _():
        gq_ref[...] = (gq_acc[...] * factor).astype(BF16)


def attend_forward(place, slopes, queries_t, keys, values, size, head_dim, pair):
    length = queries_t.shape[1]
    wide = 2 * head_dim
    along_q = pl.BlockSpec((wide, size), lambda i, me, s: (pair, i ^ me[0]))
    out_q = pl.BlockSpec((wide, size), lambda i, me, s: (0, i ^ me[0]))
    whole = pl.BlockSpec((length, wide), lambda i, me, s: (0, pair))
    return pl.pallas_call(
        functools.partial(forward_kernel, scale=LOG2E / math.sqrt(head_dim), pair=pair),
        grid_spec=pltpu.PrefetchScalarGridSpec(
            num_scalar_prefetch=2,
            grid=(length // size,),
            in_specs=[along_q, whole, whole],
            out_specs=[out_q, out_q, pl.BlockSpec((2, size), lambda i, me, s: (0, i ^ me[0]))],
            scratch_shapes=[
                pltpu.VMEM((2, size, size), F32),
                pltpu.VMEM((2, size, size), F32),
                pltpu.VMEM((wide, length), BF16),
            ],
        ),
        out_shape=[
            jax.ShapeDtypeStruct((wide, length), BF16),
            jax.ShapeDtypeStruct((wide, length), F32),
            jax.ShapeDtypeStruct((2, length), F32),
        ],
        compiler_params=pltpu.CompilerParams(vmem_limit_bytes=48 * 2**20),
        cost_estimate=pl.CostEstimate(
            flops=10 * 10**9, bytes_accessed=4 * 2**20, transcendentals=5 * 10**6
        ),
        name=f"attend_forward_{pair}",
    )(place, slopes, queries_t, keys, values)


def attend_backward(place, slopes, queries_t, keys, values, grads_t, full, logs, size, head_dim, pair):
    length = queries_t.shape[1]
    wide = 2 * head_dim
    along_k = pl.BlockSpec((size, wide), lambda i, me, s: (i ^ me[0], pair))
    out_k = pl.BlockSpec((size, wide), lambda i, me, s: (i ^ me[0], 0))
    all_q = pl.BlockSpec((wide, length), lambda i, me, s: (pair, 0))
    whole = pl.BlockSpec((wide, length), lambda i, me, s: (0, 0))
    return pl.pallas_call(
        functools.partial(
            backward_kernel,
            scale=LOG2E / math.sqrt(head_dim),
            factor=1.0 / math.sqrt(head_dim),
            pair=pair,
        ),
        grid_spec=pltpu.PrefetchScalarGridSpec(
            num_scalar_prefetch=2,
            grid=(length // size,),
            in_specs=[
                all_q,
                along_k,
                along_k,
                whole,
                whole,
                pl.BlockSpec((2, length), lambda i, me, s: (0, 0)),
            ],
            out_specs=[whole, out_k, out_k],
            scratch_shapes=[
                pltpu.VMEM((2, size, size), F32),
                pltpu.VMEM((2, size, size), F32),
                pltpu.VMEM((wide, length), F32),
                pltpu.VMEM((2, length), F32),
            ],
        ),
        out_shape=[
            jax.ShapeDtypeStruct((wide, length), BF16),
            jax.ShapeDtypeStruct((length, wide), BF16),
            jax.ShapeDtypeStruct((length, wide), BF16),
        ],
        compiler_params=pltpu.CompilerParams(vmem_limit_bytes=48 * 2**20),
        cost_estimate=pl.CostEstimate(
            flops=20 * 10**9, bytes_accessed=6 * 2**20, transcendentals=5 * 10**6
        ),
        name=f"attend_backward_{pair}",
    )(place, slopes, queries_t, keys, values, grads_t, full, logs)


def swap(value, axis, distance):
    size = lax.axis_size(axis)
    return lax.ppermute(value, axis, [(i, i ^ distance) for i in range(size)])


def after(value, *earlier):
    return lax.optimization_barrier((value,) + earlier)[0]


def exchange_blocks(parts):
    return [parts[0]] + [swap(parts[j], "tensor", j) for j in range(1, 4)]


def chip_sum(far, far_near):
    return add_rows(far, swap(far_near, "tensor", 1))


def add_rows(one, two):
    rows, width = two.shape
    tile = rows // 2
    block = pl.BlockSpec((tile, width), lambda i: (i, 0))

    def add(one_ref, two_ref, out_ref):
        out_ref[...] = (one_ref[...].astype(F32) + two_ref[...].astype(F32)).astype(BF16)

    return pl.pallas_call(
        add,
        grid=(2,),
        in_specs=[block, block],
        out_specs=block,
        out_shape=jax.ShapeDtypeStruct((rows, width), BF16),
        compiler_params=pltpu.CompilerParams(vmem_limit_bytes=32 * 2**20),
        cost_estimate=pl.CostEstimate(
            flops=rows * width, bytes_accessed=6 * rows * width, transcendentals=0
        ),
        name="add_rows",
    )(one, two)


def sum_over(value, axes, *earlier):
    for axis in axes:
        size = lax.axis_size(axis)
        distance = 1
        while distance < size:
            if distance * 4 <= size:
                one, two, three = (swap(value, axis, distance * k) for k in (1, 2, 3))
                value = after((value + one) + (two + three), *earlier)
                distance *= 4
            else:
                value = value + swap(value, axis, distance)
                distance *= 2
    return value


def ring_dp():
    count = lax.axis_size("dp")
    return list(range(0, count, 2)) + list(range(count - 1, 0, -2))


def gather_dp(shard):
    return lax.all_gather(shard, "dp", axis=0, tiled=True, axis_index_groups=[ring_dp()])


def scatter_dp(blocks):
    return lax.psum_scatter(
        blocks, "dp", scatter_dimension=0, tiled=True, axis_index_groups=[ring_dp()]
    ).astype(F32)


def at_ring(place, count):
    return jnp.where(place < count // 2, 2 * place, 2 * (count - 1 - place) + 1)


def place_in_ring(owner, count):
    return jnp.where(owner % 2 == 0, owner // 2, count - 1 - owner // 2)


def reorder(blocks, order, name):
    count = lax.axis_size("dp")
    rows, width = blocks.shape[0] // count, blocks.shape[1]

    def copy(source_ref, result_ref):
        result_ref[...] = source_ref[...]

    return pl.pallas_call(
        copy,
        grid=(count,),
        in_specs=[pl.BlockSpec((rows, width), lambda i: (order(i, count), 0))],
        out_specs=pl.BlockSpec((rows, width), lambda i: (i, 0)),
        out_shape=jax.ShapeDtypeStruct(blocks.shape, blocks.dtype),
        cost_estimate=pl.CostEstimate(
            flops=0, bytes_accessed=4 * count * rows * width, transcendentals=0
        ),
        name=name,
    )(blocks)


def ring_lanes(rows, width, index=0):
    count = lax.axis_size("dp")
    lanes = width // count
    if lanes % 128:
        return [pl.BlockSpec((rows, 256), lambda i: (index, i))]
    return [
        pl.BlockSpec((rows, lanes), lambda i, k=k: (index, at_ring(2 * i + k, count)))
        for k in range(2)
    ]


def project_kernel(ring, *refs):
    blocks, refs = refs[:4], refs[4:]
    weight_ref, bias_ref, q_ref, k_ref, v_ref, full_ref = refs
    width = q_ref.shape[0]
    step = pl.program_id(0)

    @pl.when(step == 0)
    def _():
        rows = full_ref.shape[0] // len(ring)
        for at, owner in enumerate(ring):
            full_ref[owner * rows : (owner + 1) * rows, :] = weight_ref[at * rows : (at + 1) * rows, :]

    for k, block in enumerate(blocks):

        @pl.when(step == k)
        def _(block=block):
            out = jnp.dot(block[...], full_ref[:, : 3 * width], preferred_element_type=F32)
            q_ref[...] = (out[:, :width] + bias_ref[0:1, :]).astype(BF16).T
            k_ref[...] = out[:, width : 2 * width].astype(BF16)
            v_ref[...] = (out[:, 2 * width :] + bias_ref[1:2, :]).astype(BF16)


def project(blocks, weights, bias):
    rows = blocks[0].shape[0]
    width = bias.shape[1]
    count = len(blocks)
    ring = ring_dp()

    def whole(shape):
        return pl.BlockSpec(shape, lambda i: (0, 0))

    return pl.pallas_call(
        functools.partial(project_kernel, ring),
        grid=(count,),
        in_specs=[whole(b.shape) for b in blocks] + [whole(weights.shape), whole(bias.shape)],
        out_specs=[
            pl.BlockSpec((width, rows), lambda i: (0, i)),
            pl.BlockSpec((rows, width), lambda i: (i, 0)),
            pl.BlockSpec((rows, width), lambda i: (i, 0)),
            whole(weights.shape),
        ],
        out_shape=[
            jax.ShapeDtypeStruct((width, count * rows), BF16),
            jax.ShapeDtypeStruct((count * rows, width), BF16),
            jax.ShapeDtypeStruct((count * rows, width), BF16),
            jax.ShapeDtypeStruct(weights.shape, BF16),
        ],
        compiler_params=pltpu.CompilerParams(vmem_limit_bytes=40 * 2**20),
        cost_estimate=pl.CostEstimate(
            flops=6 * count * rows * width * weights.shape[0],
            bytes_accessed=12 * 2**20,
            transcendentals=0,
        ),
        name="project",
    )(*blocks, weights, bias)


def in_ring(blocks, width, name):
    if (width // lax.axis_size("dp")) % 128:
        return reorder(blocks, at_ring, name)
    return blocks


def rows_of(value, count):
    size = value.shape[0] // count
    return [value[i * size : (i + 1) * size] for i in range(count)]


def dot(a, b, ca, cb):
    return lax.dot_general(a, b, (((ca,), (cb,)), ((), ())), preferred_element_type=F32)


def body(
    hidden_in,
    norm_gain,
    norm_shift,
    qkv_weight,
    qv_bias,
    out_weight,
    out_bias,
    up_weight,
    up_bias,
    down_weight,
    cotangent,
):
    rows, width = hidden_in.shape
    tensor_size = lax.axis_size("tensor")
    heads_wide = qkv_weight.shape[2]
    hidden_units = up_weight.shape[1]
    local_heads = HEADS // tensor_size
    head_dim = heads_wide // local_heads
    pairs = local_heads // 2
    wide = 2 * head_dim
    me = lax.axis_index("tensor").astype(jnp.int32)
    place = me.reshape(1)
    head_ids = me * local_heads + jnp.arange(local_heads, dtype=jnp.int32)
    slopes = jnp.exp2(-8.0 * (head_ids.astype(F32) + 1.0) / HEADS) * LOG2E
    part = rows // 2
    stat = functools.partial(row_call, rows=rows, width=width)
    row_f32 = jax.ShapeDtypeStruct((rows, width), F32)
    row_bf16 = jax.ShapeDtypeStruct((rows, width), BF16)
    part_bf16 = jax.ShapeDtypeStruct((part, width), BF16)
    four_f32 = jax.ShapeDtypeStruct((4, width), F32)

    first_shard = jnp.concatenate(
        [qkv_weight[0], qkv_weight[1], qkv_weight[2], out_weight.T], axis=1
    )
    second_shard = jnp.concatenate([up_weight, down_weight.T], axis=1)
    first_ring = gather_dp(first_shard)
    second_weights = gather_dp(second_shard)

    (normed,) = stat(
        first_norm_kernel, arrays=[hidden_in, norm_gain, norm_shift], outs=[row_bf16], name="norm_one"
    )
    normed_far = swap(normed, "tensor", 2)
    normed_near = swap(normed, "tensor", 1)
    normed_blocks = [normed, normed_near, normed_far, swap(normed_far, "tensor", 1)]
    grads_far = swap(cotangent, "tensor", 2)
    grads_near = swap(cotangent, "tensor", 1)
    grads_far_near = swap(grads_far, "tensor", 1)

    queries_t, keys, values, first_full = project(normed_blocks, first_ring, qv_bias)
    out_mine = first_full[:, 3 * heads_wide :]
    out_far = swap(out_mine, "tensor", 2)
    kept = []
    mixed_parts = [[] for _ in range(tensor_size)]
    received = out_far
    for pair in range(pairs):
        mixed_t, mixed_full, logs = attend_forward(
            place,
            slopes,
            queries_t
            if pair == 0
            else after(queries_t, grads_far, mixed_full),
            keys,
            values,
            rows,
            head_dim,
            pair,
        )
        if pair > 0:
            mixed_t = after(mixed_t, *received, out_far)
        kept.append((mixed_full, logs))
        parts = [mixed_t[:, j * rows : (j + 1) * rows] for j in range(tensor_size)]
        received = exchange_blocks(parts)
        for j, block in enumerate(received):
            mixed_parts[j].append(block)
    out_full = jnp.concatenate(
        [out_mine, swap(out_mine, "tensor", 1), out_far, swap(out_far, "tensor", 1)], axis=1
    )
    mixed_all = jnp.concatenate([block for group in mixed_parts for block in group], axis=0)
    attn_sum = dot(mixed_all, out_full, 0, 1)
    middle, second = stat(
        second_norm_kernel,
        arrays=[hidden_in, attn_sum, out_bias, norm_gain, norm_shift],
        outs=[row_f32, (part_bf16, part_bf16)],
        name="norm_two",
    )

    up_bias_row = up_bias.reshape(1, hidden_units)
    far_chunks = [swap(second[c], "tensor", 2) for c in range(2)]
    seconds = [[(block, 0) for block in second]]
    seconds[0] += [(swap(block, "tensor", 1), 0) for block in second]
    grads = [[(g, c) for g in (cotangent, grads_near) for c in range(2)]]
    mlp_a, back_a, active, upper, sums_up = feed(
        part, seconds[0], grads[0], second_weights, up_bias_row, jnp.zeros_like(up_bias_row), "feed_near"
    )
    actives, uppers = [active], [upper]
    far = [after(chunk, mlp_a[0]) for chunk in far_chunks]
    far = far + [swap(block, "tensor", 1) for block in far]
    seconds.append([(block, 0) for block in far])
    grads.append([(g, c) for g in (grads_far, grads_far_near) for c in range(2)])
    mlp_f, back_f, active, upper, sums_up = feed(
        part, seconds[1], grads[1], second_weights, up_bias_row, sums_up, "feed_far"
    )
    actives.append(active)
    uppers.append(upper)
    mlps = [(mlp_f[c], mlp_f[2 + c]) for c in range(2)]
    mines = [chip_sum(back_f[c], back_f[2 + c]) for c in range(2)]
    back_fars = [swap(mine, "tensor", 2) for mine in mines]
    back_near = tuple(swap(back_a[2 + c], "tensor", 1) for c in range(2))

    uppers[0] = after(uppers[0], *mines)
    grad_second_w = weight_grads(part, seconds, grads, uppers, actives)
    local_second_w = grad_second_w
    grad_second_w = scatter_dp(grad_second_w)
    grad_up_weight = grad_second_w[:, :hidden_units]
    grad_down_weight = grad_second_w[:, hidden_units:].T

    grad_middle, grad_attn, early = stat(
        second_back_kernel,
        arrays=[after(middle, local_second_w), cotangent, tuple(back_a[:2]), back_near, tuple(back_fars), norm_gain],
        outs=[row_f32, row_bf16, four_f32],
        name="norm_two_back",
    )
    mixed_grads = dot(out_full, grad_attn, 0, 1).astype(BF16)
    mlps = [lax.optimization_barrier((*m, grad_attn))[:2] for m in mlps]
    mlp_a = lax.optimization_barrier((*mlp_a, grad_attn))[:4]
    exchanged = exchange_blocks(rows_of(mixed_grads, tensor_size))
    grads_t = [
        jnp.concatenate([block[pair * wide : (pair + 1) * wide] for block in exchanged], axis=1)
        for pair in range(pairs)
    ]

    out_partial = dot(after(grad_attn, mixed_grads), mixed_all, 0, 1).astype(BF16)
    out_cols = [out_partial[:, j * heads_wide : (j + 1) * heads_wide] for j in range(tensor_size)]
    out_mine_sum = chip_sum(out_cols[2], out_cols[3])
    mlp_mine_sum = jnp.concatenate([chip_sum(m[0], m[1]) for m in mlps], axis=0)
    mlp_far = swap(mlp_mine_sum, "tensor", 2)
    out_near = swap(out_cols[1], "tensor", 1)
    out_far_sum = swap(after(out_mine_sum, mlp_far), "tensor", 2)
    mlp_near = tuple(swap(m, "tensor", 1) for m in mlp_a[2:])
    low = []
    for pair in range(pairs):
        grads_pair = grads_t[pair]
        if pair == 0:
            grads_pair = after(grads_pair, out_mine_sum, mlp_mine_sum)
        else:
            grads_pair = after(grads_pair, low[-1][0], mlp_far)
        mixed_full, logs = kept[pair]
        low.append(
            attend_backward(
                place, slopes, queries_t, keys, values, grads_pair, mixed_full, logs, rows, head_dim, pair
            )
        )
    low[-1] = lax.optimization_barrier((*low[-1], out_far_sum))[:3]
    out_sum = (
        out_cols[0].astype(F32) + out_near.astype(F32) + out_far_sum.astype(F32)
    ).astype(BF16)
    joined, column_sums = join_low(low)
    first_cols = first_full[:, : 3 * heads_wide]
    half = 2 * rows
    far_grads = dot(joined[half:], first_cols, 1, 1).astype(BF16)
    first_mine = add_rows(far_grads, swap(far_grads[rows:], "tensor", 1))
    first_far = swap(first_mine, "tensor", 2)
    send, gains = first_grads(
        normed_blocks, after(joined, first_mine), column_sums, out_sum, first_ring
    )
    first_sums = scatter_dp(after(send, grad_second_w))
    near_grads = dot(after(joined, send)[:half], first_cols, 1, 1).astype(BF16)
    first_near = swap(near_grads[rows:], "tensor", 1)

    grad_qkv = jnp.stack([first_sums[:, c * heads_wide : (c + 1) * heads_wide] for c in range(3)])
    grad_out_weight = first_sums[:, 3 * heads_wide :].T

    (grad_in,) = stat(
        first_back_kernel,
        arrays=[hidden_in, grad_middle, near_grads[:rows], first_near, first_far, norm_gain],
        outs=[row_f32],
        name="norm_one_back",
    )
    (block_out,) = stat(
        block_kernel,
        arrays=[middle, tuple(mlp_a[:2]), mlp_near, after(mlp_far, near_grads), out_bias],
        outs=[row_f32],
        name="block_out",
    )

    shift_sum = gains[:, 1]
    gain_sum = (gains[:, 0] - norm_shift[0] * shift_sum) / norm_gain[0]
    lanes = 128
    whole_sums = jnp.concatenate([early, gain_sum[None], shift_sum[None]], axis=0).reshape(-1, lanes)
    columns = column_sums[0]
    split_sums = jnp.concatenate(
        [columns[:heads_wide], columns[2 * heads_wide :], sums_up[0]]
    ).reshape(-1, lanes)
    sums = sum_over(jnp.concatenate([whole_sums, split_sums], axis=0), ("dp",), first_far, block_out, grad_up_weight, grad_down_weight)
    whole_sums = sum_over(sums[: whole_sums.shape[0]], ("tensor",)).reshape(-1, width)
    split_sums = sums[whole_sums.size // lanes :].reshape(-1)
    return (
        block_out,
        grad_in,
        jnp.stack([whole_sums[4], whole_sums[0]]),
        jnp.stack([whole_sums[5], whole_sums[1]]),
        grad_qkv,
        split_sums[: 2 * heads_wide].reshape(2, heads_wide),
        grad_out_weight,
        whole_sums[2:4],
        grad_up_weight,
        split_sums[2 * heads_wide :],
        grad_down_weight,
    )


def solution(mesh):
    return jax.shard_map(
        body,
        mesh=mesh,
        in_specs=(
            P(("dp", "tensor"), None),
            P(),
            P(),
            P(None, "dp", "tensor"),
            P(None, "tensor"),
            P("tensor", "dp"),
            P(),
            P("dp", "tensor"),
            P("tensor"),
            P("tensor", "dp"),
            P(("dp", "tensor"), None),
        ),
        out_specs=(
            P(("dp", "tensor"), None),
            P(("dp", "tensor"), None),
            P(),
            P(),
            P(None, "dp", "tensor"),
            P(None, "tensor"),
            P("tensor", "dp"),
            P(),
            P("dp", "tensor"),
            P("tensor"),
            P("tensor", "dp"),
        ),
        check_vma=False,
    )
```
